512 devices in a mesh: node: 16 (over x, y_hi, core), rep: 32 (over z, y_lo).
Axes of the slice: x: 4, y: 4 (y_hi: 2, y_lo: 2; y = y_hi * 2 + y_lo), z: 16, core: 2. Of those that a mesh axis runs over, the one named last changes fastest.
Arguments:
- tokens: bfloat16 [65536, 16384], P(('node', 'rep')), may hold values from -6 to 6
- cotangent: bfloat16 [65536, 256], P(('node', 'rep')), may hold values from -0.08984375 to 0.08984375
- weight: bfloat16 [16384, 256], P('node'), may hold values from -0.046875 to 0.046875
- gain: bfloat16 [16384], replicated, may hold values from 0.5 to 2
- exponents: int32 [16, 32, 2, 16384], P('node', 'rep'), may hold values from -13 to -8
Outputs:
- grad_weight: float32 [16384, 256], P(('node', 'rep'))
- grad_gain: float32 [16384], P(('node', 'rep'))
The draws below stay inside these ranges and needn't reach their ends.
Inputs may be any that keep to these rules, and one draw needn't show every extreme that they name: Integer exponents.
All inputs are finite; a program needn't handle non-finite values.
Results may differ from the reference program's by a relative error of at most 0.004.
Values may be sent and summed in bfloat16 or wider, within the bound.
A program may use at most 192 MiB of HBM per device.

```python
import math
import jax
import jax.numpy as jnp
from jax import lax

D = 16384
HD = 128
BLOCK = 128
TOK_DEV = 128
KV_BLOCKS = 2
TOKENS = 65536
N_NODE = 16
N_REP = 32


def with_ends(entries, own_key, smallest, high):
    longest = entries.shape.index(max(entries.shape))
    spots = []
    for shift in (0, 1):
        where = [jax.random.randint(jax.random.fold_in(own_key, axis), (), 0, length) for axis, length in enumerate(entries.shape)]
        where[longest] = (where[longest] + shift) % entries.shape[longest]
        spots.append(tuple(where))
    return entries.at[spots[0]].set(smallest).at[spots[1]].set(high)


def block_scale(stream_key, dims, split, smallest, largest):
    loudness = 1.0
    for position, parts in split:
        steps = jax.random.uniform(jax.random.fold_in(jax.random.fold_in(stream_key, 6), position), (parts,), jnp.float32, smallest / len(split), largest / len(split))
        loudness = loudness * jnp.repeat(jnp.exp(steps), dims[position] // parts).reshape((-1,) + (1,) * (len(dims) - 1 - position))
    return loudness


def scatter_about(own_key, extent, deviation, limit, pieces=(), kind=jnp.bfloat16):
    drawn = deviation * jax.random.normal(own_key, extent, jnp.float32)
    if pieces:
        drawn = drawn * block_scale(own_key, extent, pieces, -0.22, 0.18)
    return jnp.clip(drawn, -limit, limit).astype(kind)


def setup_inputs(seed: int = 0) -> dict:
    streams_of = jax.random.split(jax.random.key(seed), 6)
    tokens = scatter_about(streams_of[0], (TOKENS, D), 1.0, 6.0, ((0, 512),))
    cotangent = scatter_about(streams_of[1], (TOKENS, 2 * HD), 0.015625, 0.08984375, ((0, 512),))
    weight = scatter_about(streams_of[2], (D, 2 * HD), D ** -0.5, 0.046875, ((0, 16),))
    gain = jnp.clip(jnp.exp(jax.random.uniform(streams_of[3], (D,), jnp.float32, math.log(0.5), math.log(2.0))), 0.5, 2.0).astype(jnp.bfloat16)
    exponents = with_ends(jax.random.randint(streams_of[4], (N_NODE, N_REP, KV_BLOCKS, D), -13, -7), jax.random.fold_in(streams_of[4], 1), -13, (-7) - 1).astype(jnp.int32)
    return dict(tokens=tokens, cotangent=cotangent, weight=weight, gain=gain, exponents=exponents)


EPSILON = 1e-05
SATURATE = 448.0

def powers_of_two(exponents):
    upward = jnp.left_shift(jnp.ones_like(exponents), -exponents).astype(jnp.float32)
    return (upward, 1.0 / upward)

def device_terms(tokens, cotangent, weight, gain, exponents, node_index, rep_index):
    first = ((node_index * N_REP + rep_index) * TOK_DEV).astype(jnp.int32)
    token_rows = lax.dynamic_slice_in_dim(tokens, first, TOK_DEV, 0)
    cot_rows = lax.dynamic_slice_in_dim(cotangent, first, TOK_DEV, 0)
    widened = token_rows.astype(jnp.float32)
    inverse_rms = lax.rsqrt(lax.optimization_barrier(jnp.mean(widened * widened, axis=1)) + EPSILON)
    normed = (widened * inverse_rms[:, None] * gain.astype(jnp.float32)[None, :]).astype(jnp.bfloat16)
    partial_value = lax.dot_general(normed, cot_rows, (((0,), (0,)), ((), ())), preferred_element_type=jnp.float32)
    to_wire, from_wire = powers_of_two(exponents[node_index, rep_index])
    scaled = partial_value.reshape(D, KV_BLOCKS, BLOCK) * to_wire.T[:, :, None]
    quantized = jnp.clip(scaled, -SATURATE, SATURATE).astype(jnp.bfloat16)
    restored = (quantized.astype(jnp.float32) * from_wire.T[:, :, None]).reshape(D, 2 * HD)
    projected = jnp.dot(cot_rows, weight.T, preferred_element_type=jnp.float32)
    gain_term = lax.optimization_barrier(jnp.sum(projected * widened * inverse_rms[:, None], axis=0))
    return (restored, gain_term)

def reference(tokens, cotangent, weight, gain, exponents):

    def replica_step(rep_index, carry):
        total, gain_total = carry

        def node_step(node_index, inner):
            node_sum, gain_acc = inner
            restored, gain_term = device_terms(tokens, cotangent, weight, gain, exponents, jnp.asarray(node_index).astype(jnp.int32), jnp.asarray(rep_index).astype(jnp.int32))
            return (node_sum + restored, gain_acc + gain_term)
        start = (jnp.zeros((D, 2 * HD), jnp.float32), gain_total)
        node_sum, gain_total = lax.fori_loop(0, N_NODE, node_step, start)
        return (total + node_sum, gain_total)
    begin = (jnp.zeros((D, 2 * HD), jnp.float32), jnp.zeros((D,), jnp.float32))
    grad_weight, grad_gain = lax.fori_loop(0, N_REP, replica_step, begin)
    return (grad_weight, grad_gain)
```

```python
import functools

import jax
import jax.numpy as jnp
from jax import lax
from jax.experimental import pallas as pl
from jax.experimental.pallas import tpu as pltpu
from jax.sharding import PartitionSpec as P

EPSILON = 1e-05
SATURATE = 448.0
MESH = pl.DeviceIdType.MESH
F32 = jnp.float32
BF16 = jnp.bfloat16


def device(x, y, z, core):
    return ((x * 2 + lax.div(y, 2)) * 2 + core, z * 2 + lax.rem(y, 2))


def kernel(
    width, slab, nz,
    tok_hbm, cot_hbm, w_hbm, gain_hbm, exp_hbm,
    gw_ref, gg_ref,
    tokv, cotv, wv, gainv, expv, sibexp, invb, wall,
    usend, uown, urecv,
    p1, relp1, relm1, inm1, inp1,
    p2, relp2, relm2, inm2, inp2,
    hbuf, hx, hcross, hsum, zsrc, zrecv, fin, outt, hrow,
    loc_sem, tok_sem, core_s, core_r, exp_s, exp_r,
    agx_s, agx_r, agf_s, agf_r, agc_s, agc_r, ags_s, ags_r,
    st1_s, st1_r, st2_s, st2_r, hx_s, hx_r, hc_s, hc_r, z_s, z_r, fin_s, fin_r,
):
    node, rep = lax.axis_index("node"), lax.axis_index("rep")
    core = lax.rem(node, 2)
    yh = lax.rem(lax.div(node, 2), 2)
    x = lax.div(node, 4)
    yl = lax.rem(rep, 2)
    z = lax.div(rep, 2)
    y = yh * 2 + yl
    zl, zh = lax.rem(z, 2), lax.div(z, 2)
    zpair = z + 1 - 2 * zl
    ysame = yh * 2 + 1 - yl
    ycross = (1 - yh) * 2 + 1 - yl
    xs = [lax.rem(x + d, 4) for d in range(4)]
    ys = [lax.rem(y + d, 4) for d in range(4)]
    sibling = device(x, y, z, 1 - core)
    tiles = slab // 128

    def remote(src, dst, send, recv, where):
        return pltpu.make_async_remote_copy(
            src_ref=src, dst_ref=dst, send_sem=send, recv_sem=recv, device_id=where, device_id_type=MESH
        )

    loads = [
        pltpu.make_async_copy(w_hbm, wv, loc_sem.at[0]),
        pltpu.make_async_copy(cot_hbm, cotv, loc_sem.at[1]),
        pltpu.make_async_copy(gain_hbm, gainv, loc_sem.at[2]),
        pltpu.make_async_copy(exp_hbm, expv, loc_sem.at[3]),
    ]
    for load in loads:
        load.start()

    def token_load(s):
        at = pl.multiple_of(s * slab, slab)
        return pltpu.make_async_copy(tok_hbm.at[:, pl.ds(at, slab)], tokv.at[s], tok_sem.at[s])

    @pl.loop(0, 16)
    def _(s):
        token_load(s).start()

    barrier = pltpu.get_barrier_semaphore()
    partners = [
        sibling,
        device(xs[1], y, z, core), device(xs[2], y, z, core), device(xs[3], y, z, core),
        device(x, ys[1], z, core), device(x, ys[3], z, core),
        device(x, ysame, zpair, core),
    ]
    for where in partners:
        pl.semaphore_signal(barrier, inc=1, device_id=where, device_id_type=MESH)

    @pl.loop(1, nz)
    def _(d):
        pl.semaphore_signal(
            barrier, inc=1, device_id=device(x, y, lax.rem(z + d, nz), core), device_id_type=MESH
        )

    loads[0].wait()
    for t in range(tiles):
        for h in range(2):
            block = wv[t * 128 : (t + 1) * 128, h * 128 : (h + 1) * 128].astype(F32)
            wall[x, yh, h * 8 : (h + 1) * 8, :, t * 128 : (t + 1) * 128] = (
                block.T.astype(BF16).reshape(8, 16, 128)
            )
    loads[1].wait()
    loads[2].wait()
    loads[3].wait()
    pl.semaphore_wait(barrier, len(partners) + nz - 1)

    xplus, xminus = device(xs[1], y, z, core), device(xs[3], y, z, core)
    yplus, yminus = device(x, ys[1], z, core), device(x, ys[3], z, core)
    cross, same = device(x, ycross, z, core), device(x, ysame, z, core)
    half = pl.ds(0, 8), pl.ds(8, 8)
    hy = lax.rem(yh + yl, 2) * 8
    yhalf = pl.ds(hy, 8)

    def agx(k):
        return remote(wall.at[x, yh], wall.at[x, yh], agx_s.at[k], agx_r.at[k], (xplus, xminus)[k])

    def agf(k):
        ref = wall.at[xs[3 if k == 0 else 1], yh, half[k]]
        return remote(ref, ref, agf_s.at[k], agf_r.at[k], (xplus, xminus)[k])

    def agc(d):
        ref = wall.at[xs[d], yh, yhalf]
        return remote(ref, ref, agc_s.at[d], agc_r.at[d], cross)

    def ags(d):
        ref = wall.at[xs[d], 1 - yh, yhalf]
        return remote(ref, ref, ags_s.at[d], ags_r.at[d], same)

    agx(0).start()
    agx(1).start()
    agc(0).start()
    exps = remote(expv, sibexp, exp_s, exp_r, sibling)
    exps.start()

    def square(s, total):
        token_load(s).wait()
        for t in range(tiles):
            v = tokv[s, :, t * 128 : (t + 1) * 128].astype(F32)
            total = total + v * v
        return total

    total = lax.fori_loop(0, 16, square, jnp.zeros((128, 128), F32))
    inverse = lax.rsqrt(jnp.sum(total, axis=1, keepdims=True) * (1.0 / width) + EPSILON)
    step = min(slab, 256)
    invb[...] = jnp.broadcast_to(inverse, (128, step))
    cot_t = cotv[...].astype(F32).T.astype(BF16)

    def partial_slab(i, parity, out):
        s = i * 2 + parity
        for t in range(slab // step):
            g = gainv[:, pl.ds(pl.multiple_of(s * slab + t * step, step), step)].astype(F32)
            v = tokv[s, :, t * step : (t + 1) * step].astype(F32)
            normed = (v * invb[...] * g).astype(BF16)
            part = jnp.dot(cot_t, normed, preferred_element_type=F32)
            out[i, :, :, t * step : (t + 1) * step] = part.astype(BF16).reshape(16, 16, step)

    def core_copy(i):
        return remote(usend.at[i], urecv.at[i], core_s.at[i], core_r.at[i], sibling)

    @pl.loop(0, 8)
    def _(i):
        partial_slab(i, 1 - core, usend)
        core_copy(i).start()

    @pl.loop(0, 8)
    def _(i):
        partial_slab(i, core, uown)

    agx(0).wait_recv()
    agf(0).start()
    agc(3).start()
    agx(1).wait_recv()
    agf(1).start()
    agc(1).start()
    agc(0).wait_recv()
    ags(0).start()

    exps.wait_recv()
    parity_at = core * slab

    def threshold(ref, k, i):
        at = pl.multiple_of(i * 2 * slab + parity_at, slab)
        e = ref[k : k + 1, pl.ds(at, slab)]
        return jnp.left_shift(jnp.ones_like(e), e + 30).astype(F32) * (SATURATE * 2.0**-30)

    @pl.loop(0, 8)
    def _(i):
        core_copy(i).wait_recv()
        px, pyh = lax.div(i, 2), lax.rem(i, 2)
        for k in range(2):
            mine, theirs = threshold(expv, k, i), threshold(sibexp, k, i)
            for g in range(k * 8, k * 8 + 8):
                a = uown[i, g].astype(F32)
                b = urecv[i, g].astype(F32)
                a = jnp.minimum(jnp.maximum(a, -mine), mine)
                b = jnp.minimum(jnp.maximum(b, -theirs), theirs)
                q, lg = g // 4, g % 4
                value = (a + b).astype(BF16)
                if q % 2 == 0:
                    p1[q, px, lg // 2, pyh * 2 + lg % 2] = value
                else:
                    p1[q, pyh * 2 + lg // 2, lg % 2, px] = value

    def ring(q, stage):
        along_x = (q + stage) % 2 == 0
        plus, minus = (xplus, xminus) if along_x else (yplus, yminus)
        at = xs if along_x else ys
        p, relp, relm, inm, inp, ss, rs = (
            (p1, relp1, relm1, inm1, inp1, st1_s, st1_r),
            (p2, relp2, relm2, inm2, inp2, st2_s, st2_r),
        )[stage]

        def sem(k):
            return ss.at[q * 6 + k], rs.at[q * 6 + k]

        def copy(k):
            src, dst, where = (
                (p.at[q, at[2], 0], relp.at[q], plus),
                (p.at[q, at[2], 1], relm.at[q], minus),
                (p.at[q, at[1], 1], inm.at[q, 1], plus),
                (p.at[q, at[3], 0], inp.at[q, 0], minus),
                (p.at[q, at[1], 0], inm.at[q, 0], plus),
                (p.at[q, at[3], 1], inp.at[q, 1], minus),
            )[k]
            return remote(src, dst, *sem(k), where)

        return copy, at, p, relp, relm

    def ring_open(q, stage):
        copy = ring(q, stage)[0]
        for k in range(4):
            copy(k).start()

    def ring_relay(q, stage):
        copy, at, p, relp, relm = ring(q, stage)
        for c, d, h, rel in ((0, 1, 0, relp), (1, 3, 1, relm)):
            copy(c).wait_recv()
            if stage == 0:
                for m in range(4):
                    p[q, at[d], h, m] = (p[q, at[d], h, m].astype(F32) + rel[q, m].astype(F32)).astype(BF16)
            else:
                p[q, at[d], h] = (p[q, at[d], h].astype(F32) + rel[q].astype(F32)).astype(BF16)
            copy(4 + c).start()

    def ring_wait(q, stage):
        copy = ring(q, stage)[0]
        for k in range(2, 6):
            copy(k).wait_recv()

    for q in range(4):
        ring_open(q, 0)

    agf(0).wait_recv()
    agf(1).wait_recv()
    agc(2).start()
    agc(3).wait_recv()
    ags(3).start()
    agc(1).wait_recv()
    ags(1).start()

    for q in range(4):
        ring_relay(q, 0)

    agc(2).wait_recv()
    ags(2).start()
    for d in range(4):
        ags(d).wait_recv()

    @pl.loop(0, 8)
    def _(i):
        px, pyh = lax.div(i, 2), lax.rem(i, 2)
        total = jnp.zeros((16, slab), F32)
        for g in range(16):
            u = uown[i, g].astype(F32) + urecv[i, g].astype(F32)
            total = total + u * wall[px, pyh, g].astype(F32)
        at = pl.multiple_of(i * 2 * slab + parity_at, slab)
        row = jnp.sum(total, axis=0, keepdims=True) / gainv[:, pl.ds(at, slab)].astype(F32)
        if tiles < 8:
            hbuf[px, pyh] = jnp.zeros((8, 128), F32)
        for t in range(tiles):
            hbuf[px, pyh, t : t + 1, :] = row[:, t * 128 : (t + 1) * 128]

    def hx_copy(d):
        return remote(
            hbuf.at[xs[d]], hx.at[d], hx_s.at[d], hx_r.at[d], device(xs[d], y, z, core)
        )

    for d in range(1, 4):
        hx_copy(d).start()

    for q in range(4):
        ring_wait(q, 0)
        own = xs[0] if q % 2 == 0 else ys[0]
        for h in range(2):
            for m in range(4):
                value = (
                    p1[q, own, h, m].astype(F32) + inm1[q, h, m].astype(F32) + inp1[q, h, m].astype(F32)
                ).astype(BF16)
                if q % 2 == 0:
                    p2[q, (m // 2) * 2 + h, m % 2] = value
                else:
                    p2[q, m, h] = value
        ring_open(q, 1)

    for d in range(1, 4):
        hx_copy(d).wait_recv()
    hx[0] = hbuf[x] + hx[1] + hx[2] + hx[3]
    hc_copy = remote(hx.at[0, 1 - yh], hcross, hc_s, hc_r, cross)
    hc_copy.start()

    for q in range(4):
        ring_relay(q, 1)

    hc_copy.wait_recv()
    h_value = hx[0, yh] + hcross[...]
    hi = h_value.astype(BF16).astype(F32)
    hsum[0:8] = hi
    hsum[8:16] = h_value - hi
    split = hsum[...].astype(BF16)
    for zp in range(nz):
        zsrc[zp, 4] = split

    for q in range(4):
        ring_wait(q, 1)
        own = xs[0] if q % 2 == 1 else ys[0]
        for h in range(2):
            value = (
                p2[q, own, h].astype(F32) + inm2[q, h].astype(F32) + inp2[q, h].astype(F32)
            ).astype(BF16)
            for t in range(tiles):
                zsrc[t * 2 + h, q] = value[:, t * 128 : (t + 1) * 128]

    def z_copy(d):
        there = lax.rem(z + d, nz)
        return remote(zsrc.at[there], zrecv.at[d], z_s.at[d], z_r.at[d], device(x, y, there, core))

    @pl.loop(1, nz)
    def _(d):
        z_copy(d).start()

    mine = yl * 2 + zl
    fin[mine] = zsrc[z].astype(F32)

    @pl.loop(1, nz)
    def _(d):
        z_copy(d).wait_recv()
        fin[mine] += zrecv[d].astype(F32)

    ends = [device(x, y, zpair, core), device(x, ysame, z, core), device(x, ysame, zpair, core)]
    fin_copies = [
        remote(fin.at[mine], fin.at[mine], fin_s.at[k], fin_r.at[k], ends[k]) for k in range(3)
    ]
    for copy in fin_copies:
        copy.start()

    for k in range(2):
        agx(k).wait_send()
        agf(k).wait_send()
    for d in range(4):
        agc(d).wait_send()
        ags(d).wait_send()
    exps.wait_send()

    @pl.loop(0, 8)
    def _(i):
        core_copy(i).wait_send()

    for stage in range(2):
        for q in range(4):
            copy = ring(q, stage)[0]
            for k in range(6):
                copy(k).wait_send()
    for d in range(1, 4):
        hx_copy(d).wait_send()
    hc_copy.wait_send()

    @pl.loop(1, nz)
    def _(d):
        z_copy(d).wait_send()

    for copy in fin_copies:
        copy.wait()
    place = zl * 2 + yl
    for q in range(4):
        block = fin[:, q].reshape(64, 128)
        outt[:, q * 64 : (q + 1) * 64] = block.T
    gw_ref[...] = outt[pl.ds(pl.multiple_of(place * 32, 32), 32), :]
    both = fin[mine, 4] + fin[(1 - yl) * 2 + zl, 4]
    h_all = both[0:8] + both[8:16]
    hrow[...] = pltpu.roll(h_all, lax.rem(128 - place * 32, 128), 1)
    gg_ref[...] = hrow[pl.ds(zh, 1), 0:32]


def body(tokens, cotangent, weight, gain, exponents):
    width = tokens.shape[1]
    nz = lax.axis_size("rep") // 2
    slab = width // 16
    dma = pltpu.SemaphoreType.DMA
    vmem = pltpu.VMEM
    scratch = [
        vmem((16, 128, slab), BF16),
        vmem((128, 256), BF16),
        vmem((slab, 256), BF16),
        vmem((1, width), BF16),
        vmem((2, width), jnp.int32),
        vmem((2, width), jnp.int32),
        vmem((128, min(slab, 256)), F32),
        vmem((4, 2, 16, 16, slab), BF16),
        vmem((8, 16, 16, slab), BF16),
        vmem((8, 16, 16, slab), BF16),
        vmem((8, 16, 16, slab), BF16),
        vmem((4, 4, 2, 4, 16, slab), BF16),
        vmem((4, 4, 16, slab), BF16),
        vmem((4, 4, 16, slab), BF16),
        vmem((4, 2, 4, 16, slab), BF16),
        vmem((4, 2, 4, 16, slab), BF16),
        vmem((4, 4, 2, 16, slab), BF16),
        vmem((4, 16, slab), BF16),
        vmem((4, 16, slab), BF16),
        vmem((4, 2, 16, slab), BF16),
        vmem((4, 2, 16, slab), BF16),
        vmem((4, 2, 8, 128), F32),
        vmem((4, 2, 8, 128), F32),
        vmem((8, 128), F32),
        vmem((16, 128), F32),
        vmem((nz, 5, 16, 128), BF16),
        vmem((nz, 5, 16, 128), BF16),
        vmem((4, 5, 16, 128), F32),
        vmem((128, 256), F32),
        vmem((8, 128), F32),
        dma((4,)), dma((16,)), dma((8,)), dma((8,)), dma, dma,
        dma((2,)), dma((2,)), dma((2,)), dma((2,)), dma((4,)), dma((4,)), dma((4,)), dma((4,)),
        dma((24,)), dma((24,)), dma((24,)), dma((24,)), dma((4,)), dma((4,)), dma, dma,
        dma((nz,)), dma((nz,)), dma((3,)), dma((3,)),
    ]
    any_space = pl.BlockSpec(memory_space=pl.ANY)
    grad_weight, grad_gain = pl.pallas_call(
        functools.partial(kernel, width, slab, nz),
        out_shape=(
            jax.ShapeDtypeStruct((32, 256), F32),
            jax.ShapeDtypeStruct((1, 32), F32),
        ),
        in_specs=[any_space] * 5,
        out_specs=(pl.BlockSpec(memory_space=pltpu.VMEM),) * 2,
        scratch_shapes=scratch,
        compiler_params=pltpu.CompilerParams(
            collective_id=0, has_side_effects=True, vmem_limit_bytes=48 * 2**20
        ),
    )(tokens, cotangent, weight, gain.reshape(1, width), exponents.reshape(2, width))
    return (grad_weight, grad_gain.reshape(32))


def solution(mesh):
    placed = (
        P(("node", "rep"), None),
        P(("node", "rep"), None),
        P("node", None),
        P(),
        P("node", "rep", None, None),
    )
    return jax.shard_map(
        body,
        mesh=mesh,
        in_specs=placed,
        out_specs=(P(("node", "rep"), None), P(("node", "rep"))),
        check_vma=False,
    )
```

```python
import functools

import jax
import jax.numpy as jnp
from jax import lax
from jax.experimental import pallas as pl
from jax.experimental.pallas import tpu as pltpu
from jax.sharding import PartitionSpec as P

EPSILON = 1e-05
SATURATE = 448.0
MESH = pl.DeviceIdType.MESH
F32 = jnp.float32
BF16 = jnp.bfloat16


def device(x, y, z, core):
    return ((x * 2 + lax.div(y, 2)) * 2 + core, z * 2 + lax.rem(y, 2))


def kernel(
    width, slab, nz,
    tok_hbm, cot_hbm, w_hbm, gain_hbm, exp_hbm,
    gw_ref, gg_ref,
    tokv, cotv, wv, gainv, expv, sibexp, invb, wall,
    usend, uown, urecv,
    p1, relp1, relm1, inm1, inp1,
    p2, in2,
    hbuf, hx, hcross, zsrc0, zsrc1, zrecv0, zrecv1, zhsrc, zhrecv, fin, outt, hrow,
    heard, loc_sem, tok_sem, core_s, core_r, exp_s, exp_r,
    agx_s, agx_r, agf_s, agf_r, agc_s, agc_r, ags_s, ags_r, agz_s, agz_r,
    st1_s, st1_r, st2_s, st2_r, hx_s, hx_r, hc_s, hc_r, z_s, z_r, zh_s, zh_r, fin_s, fin_r,
):
    node, rep = lax.axis_index("node"), lax.axis_index("rep")
    core = lax.rem(node, 2)
    yh = lax.rem(lax.div(node, 2), 2)
    x = lax.div(node, 4)
    yl = lax.rem(rep, 2)
    z = lax.div(rep, 2)
    y = yh * 2 + yl
    zl, zh = lax.rem(z, 2), lax.div(z, 2)
    zpair = z + 1 - 2 * zl
    ysame = yh * 2 + 1 - yl
    ycross = (1 - yh) * 2 + 1 - yl
    xs = [lax.rem(x + d, 4) for d in range(4)]
    ys = [lax.rem(y + d, 4) for d in range(4)]
    sibling = device(x, y, z, 1 - core)
    tiles = slab // 128

    def remote(src, dst, send, recv, where):
        return pltpu.make_async_remote_copy(
            src_ref=src, dst_ref=dst, send_sem=send, recv_sem=recv, device_id=where, device_id_type=MESH
        )

    loads = [
        pltpu.make_async_copy(w_hbm, wv, loc_sem.at[0]),
        pltpu.make_async_copy(cot_hbm, cotv, loc_sem.at[1]),
        pltpu.make_async_copy(gain_hbm, gainv, loc_sem.at[2]),
        pltpu.make_async_copy(exp_hbm, expv, loc_sem.at[3]),
    ]
    for load in loads:
        load.start()

    def token_load(s):
        at = pl.multiple_of(s * slab, slab)
        return pltpu.make_async_copy(tok_hbm.at[:, pl.ds(at, slab)], tokv.at[s], tok_sem.at[s])

    @pl.loop(0, 16)
    def _(s):
        token_load(s).start()

    barrier = pltpu.get_barrier_semaphore()
    zplus, zminus = lax.rem(z + 1, nz), lax.rem(z + nz - 1, nz)
    partners = [
        sibling,
        device(xs[1], y, z, core), device(xs[2], y, z, core), device(xs[3], y, z, core),
        device(x, ys[1], z, core), device(x, ys[2], z, core), device(x, ys[3], z, core),
        device(x, y, zplus, core), device(x, y, zminus, core),
    ]
    for where in partners:
        pl.semaphore_signal(barrier, inc=1, device_id=where, device_id_type=MESH)

    def tell(k):
        far = 2**k
        listeners = [device(x, y, lax.rem(z + far, nz), core), device(x, y, lax.rem(z + nz - far, nz), core)]
        if k == 0:
            listeners.append(device(x, ysame, z, core))
        if far == 1 or 2 * far < nz:
            for where in listeners:
                pl.semaphore_signal(heard.at[k], inc=1, device_id=where, device_id_type=MESH)

    def hear(k):
        if 2**k == 1 or 2 ** (k + 1) < nz:
            pl.semaphore_wait(heard.at[k], 3 if k == 0 else 2)

    loads[0].wait()
    for t in range(tiles):
        for h in range(2):
            block = wv[t * 128 : (t + 1) * 128, h * 128 : (h + 1) * 128].astype(F32)
            wall[x, yh, h * 8 : (h + 1) * 8, :, t * 128 : (t + 1) * 128] = (
                block.T.astype(BF16).reshape(8, 16, 128)
            )
    loads[1].wait()
    loads[2].wait()
    loads[3].wait()

    xplus, xminus = device(xs[1], y, z, core), device(xs[3], y, z, core)
    yplus, yminus = device(x, ys[1], z, core), device(x, ys[3], z, core)
    cross, same = device(x, ycross, z, core), device(x, ysame, z, core)
    hy = lax.rem(yh + yl, 2)
    first = zl * 8
    yquarter = pl.ds(first + hy * 4, 4)

    def agx(d, k):
        ref = wall.at[x, yh, pl.ds(first + 4 * k, 4)]
        n = d - 1 + k
        return remote(ref, ref, agx_s.at[n], agx_r.at[n], device(xs[d], y, z, core))

    def agf(k):
        ref = wall.at[xs[3 - 2 * k], yh, pl.ds(first + 4 * k, 4)]
        return remote(ref, ref, agf_s.at[k], agf_r.at[k], (xplus, xminus)[k])

    def agc(d):
        ref = wall.at[xs[d], yh, yquarter]
        return remote(ref, ref, agc_s.at[d], agc_r.at[d], cross)

    def ags(d):
        ref = wall.at[xs[d], 1 - yh, yquarter]
        return remote(ref, ref, ags_s.at[d], ags_r.at[d], same)

    def agz(k, d, e):
        ref = wall.at[xs[d], yh if e == 0 else 1 - yh, pl.ds(first + 4 * k, 4)]
        n = k * 8 + e * 4 + d
        there = device(x, y, lax.rem(z + nz + 2 * k - 1, nz), core)
        return remote(ref, ref, agz_s.at[n], agz_r.at[n], there)

    z_sends = [(k, d, e) for k in range(2) for d in range(4) for e in range(2) if d + e]

    def from_x(k):
        agx(1, k).wait_recv()
        agx(3, k).wait_recv()
        agf(k).start()
        agz(k, 3, 0).start()
        agz(k, 1, 0).start()

    def from_opposite():
        for k in range(2):
            agf(k).wait_recv()
            agz(k, 2, 0).start()
        agc(2).start()

    def from_cross(d):
        agc(d).wait_recv()
        ags(d).start()
        agz(hy, d, 1).start()

    def from_same(d):
        ags(d).wait_recv()
        agz(1 - hy, d, 1).start()

    def square(s, total):
        token_load(s).wait()
        for t in range(tiles):
            v = tokv[s, :, t * 128 : (t + 1) * 128].astype(F32)
            total = total + v * v
        return total

    total = lax.fori_loop(0, 16, square, jnp.zeros((128, 128), F32))
    inverse = lax.rsqrt(jnp.sum(total, axis=1, keepdims=True) * (1.0 / width) + EPSILON)
    step = min(slab, 256)
    invb[...] = jnp.broadcast_to(inverse, (128, step))
    cot_t = cotv[...].astype(F32).T.astype(BF16)

    def partial_slab(i, parity, out):
        s = i * 2 + parity
        for t in range(slab // step):
            g = gainv[:, pl.ds(pl.multiple_of(s * slab + t * step, step), step)].astype(F32)
            v = tokv[s, :, t * step : (t + 1) * step].astype(F32)
            normed = (v * invb[...] * g).astype(BF16)
            part = jnp.dot(cot_t, normed, preferred_element_type=F32)
            out[i, :, :, t * step : (t + 1) * step] = part.astype(BF16).reshape(16, 16, step)

    def core_copy(q):
        rows = pl.ds(4 * q, 4)
        return remote(usend.at[:, rows], urecv.at[:, rows], core_s.at[q], core_r.at[q], sibling)

    exps = remote(expv, sibexp, exp_s, exp_r, sibling)

    @pl.loop(0, 8)
    def _(i):
        partial_slab(i, 1 - core, usend)

    pl.semaphore_wait(barrier, len(partners))
    tell(0)
    exps.start()
    core_copy(0).start()
    agx(1, 0).start()
    agx(3, 0).start()
    agx(1, 1).start()
    agx(3, 1).start()
    agc(0).start()
    core_copy(1).start()
    core_copy(2).start()
    core_copy(3).start()

    @pl.loop(0, 8)
    def _(i):
        partial_slab(i, core, uown)

    hear(0)
    tell(1)

    exps.wait_recv()
    parity_at = core * slab

    def threshold(ref, k, i):
        at = pl.multiple_of(i * 2 * slab + parity_at, slab)
        e = ref[k : k + 1, pl.ds(at, slab)]
        return jnp.left_shift(jnp.ones_like(e), e + 30).astype(F32) * (SATURATE * 2.0**-30)

    def combine(q):
        k = q // 2
        core_copy(q).wait_recv()

        @pl.loop(0, 8)
        def _(i):
            px, pyh = lax.div(i, 2), lax.rem(i, 2)
            mine, theirs = threshold(expv, k, i), threshold(sibexp, k, i)
            for lg in range(4):
                a = uown[i, q * 4 + lg].astype(F32)
                b = urecv[i, q * 4 + lg].astype(F32)
                a = jnp.minimum(jnp.maximum(a, -mine), mine)
                b = jnp.minimum(jnp.maximum(b, -theirs), theirs)
                value = (a + b).astype(BF16)
                if q % 2 == 0:
                    p1[q, px, lg // 2, pyh * 2 + lg % 2] = value
                else:
                    p1[q, pyh * 2 + lg // 2, lg % 2, px] = value

    def ring(q, k):
        plus, minus = (xplus, xminus) if q % 2 == 0 else (yplus, yminus)
        at = xs if q % 2 == 0 else ys
        src, dst, where = (
            (p1.at[q, at[2], 0], relp1.at[q], plus),
            (p1.at[q, at[2], 1], relm1.at[q], minus),
            (p1.at[q, at[1], 1], inm1.at[q, 1], plus),
            (p1.at[q, at[3], 0], inp1.at[q, 0], minus),
            (p1.at[q, at[1], 0], inm1.at[q, 0], plus),
            (p1.at[q, at[3], 1], inp1.at[q, 1], minus),
        )[k]
        return remote(src, dst, st1_s.at[q * 6 + k], st1_r.at[q * 6 + k], where)

    def ring_open(q):
        for k in range(4):
            ring(q, k).start()

    def ring_relay(q):
        at = xs if q % 2 == 0 else ys
        for c, d, h, rel in ((0, 1, 0, relp1), (1, 3, 1, relm1)):
            ring(q, c).wait_recv()
            for m in range(4):
                p1[q, at[d], h, m] = (p1[q, at[d], h, m].astype(F32) + rel[q, m].astype(F32)).astype(BF16)
            ring(q, 4 + c).start()

    def direct(q, d):
        there = device(xs[d], y, z, core) if q % 2 == 1 else device(x, ys[d], z, core)
        at = xs if q % 2 == 1 else ys
        n = q * 4 + d
        return remote(p2.at[q, at[d]], in2.at[q, d], st2_s.at[n], st2_r.at[n], there)

    def ring_close(q):
        for k in range(2, 6):
            ring(q, k).wait_recv()
        own = xs[0] if q % 2 == 0 else ys[0]
        for h in range(2):
            for m in range(4):
                value = (
                    p1[q, own, h, m].astype(F32) + inm1[q, h, m].astype(F32) + inp1[q, h, m].astype(F32)
                ).astype(BF16)
                if q % 2 == 0:
                    p2[q, (m // 2) * 2 + h, m % 2] = value
                else:
                    p2[q, m, h] = value
        for d in (2, 1, 3):
            direct(q, d).start()

    def gain_terms():
        @pl.loop(0, 8)
        def _(i):
            px, pyh = lax.div(i, 2), lax.rem(i, 2)
            total = jnp.zeros((16, slab), F32)
            for g in range(16):
                u = uown[i, g].astype(F32) + urecv[i, g].astype(F32)
                total = total + u * wall[px, pyh, g].astype(F32)
            at = pl.multiple_of(i * 2 * slab + parity_at, slab)
            row = jnp.sum(total, axis=0, keepdims=True) / gainv[:, pl.ds(at, slab)].astype(F32)
            if tiles < 8:
                hbuf[px, pyh] = jnp.zeros((8, 128), F32)
            for t in range(tiles):
                hbuf[px, pyh, t : t + 1, :] = row[:, t * 128 : (t + 1) * 128]

    def hx_copy(d):
        return remote(
            hbuf.at[xs[d]], hx.at[d], hx_s.at[d], hx_r.at[d], device(xs[d], y, z, core)
        )

    def finish(q):
        own = xs[0] if q % 2 == 1 else ys[0]
        for d in (1, 2, 3):
            direct(q, d).wait_recv()
        zsrc = (zsrc0, zsrc1)[q // 2]
        for h in range(2):
            value = (
                p2[q, own, h].astype(F32)
                + in2[q, 1, h].astype(F32) + in2[q, 2, h].astype(F32) + in2[q, 3, h].astype(F32)
            ).astype(BF16)
            for t in range(tiles):
                zsrc[t * 2 + h, q % 2] = value[:, t * 128 : (t + 1) * 128]

    def z_copy(b, d):
        there = lax.rem(z + d, nz)
        src, dst = ((zsrc0, zrecv0), (zsrc1, zrecv1))[b]
        n = b * nz + d
        return remote(src.at[there], dst.at[d], z_s.at[n], z_r.at[n], device(x, y, there, core))

    def zh_copy(d):
        there = lax.rem(z + d, nz)
        return remote(zhsrc, zhrecv.at[d], zh_s.at[d], zh_r.at[d], device(x, y, there, core))

    def z_send(b):
        @pl.loop(1, nz)
        def _(d):
            z_copy(b, d).start()

    hc_copy = remote(hx.at[0, 1 - yh], hcross, hc_s, hc_r, cross)

    def gain_start():
        for k, d, e in z_sends:
            agz(k, d, e).wait_recv()
        gain_terms()
        for d in range(1, 4):
            hx_copy(d).start()

    def gain_cross():
        for d in range(1, 4):
            hx_copy(d).wait_recv()
        hx[0] = hbuf[x] + hx[1] + hx[2] + hx[3]
        hc_copy.start()

    def gain_z():
        hc_copy.wait_recv()
        zhsrc[...] = hx[0, yh] + hcross[...]

        @pl.loop(1, nz)
        def _(d):
            zh_copy(d).start()

    from_x(0)
    combine(0)
    ring_open(0)
    from_x(1)
    agc(3).start()
    agc(1).start()
    combine(1)
    ring_open(1)
    from_cross(0)
    combine(2)
    combine(3)
    hear(1)
    tell(2)
    ring_relay(0)
    ring_relay(1)
    from_opposite()
    ring_open(2)
    ring_open(3)
    for d in (3, 1):
        from_cross(d)
    from_same(0)
    ring_relay(2)
    ring_relay(3)
    from_cross(2)
    for d in (3, 1):
        from_same(d)
    ring_close(0)
    ring_close(1)
    from_same(2)
    hear(2)
    ring_close(2)
    ring_close(3)
    finish(0)
    finish(1)
    z_send(0)
    finish(2)
    finish(3)
    z_send(1)
    gain_start()
    gain_cross()
    gain_z()

    mine = yl * 2 + zl
    fin[mine, 0:2] = zsrc0[z].astype(F32)
    fin[mine, 2:4] = zsrc1[z].astype(F32)
    fin[mine, 4, 0:8] = zhsrc[...]
    fin[mine, 4, 8:16] = jnp.zeros((8, 128), F32)

    for b in range(2):

        @pl.loop(1, nz)
        def _(d):
            z_copy(b, d).wait_recv()
            if b == 0:
                fin[mine, 0:2] += zrecv0[d].astype(F32)
            else:
                fin[mine, 2:4] += zrecv1[d].astype(F32)

    @pl.loop(1, nz)
    def _(d):
        zh_copy(d).wait_recv()
        fin[mine, 4, 0:8] += zhrecv[d]

    ends = [device(x, y, zpair, core), device(x, ysame, z, core), device(x, ysame, zpair, core)]
    fin_copies = [
        remote(fin.at[mine], fin.at[mine], fin_s.at[k], fin_r.at[k], ends[k]) for k in range(3)
    ]
    for copy in fin_copies:
        copy.start()

    for d in range(1, 4):
        hx_copy(d).wait_send()
    for k in range(2):
        agx(1, k).wait_send()
        agx(3, k).wait_send()
        agf(k).wait_send()
    for d in range(4):
        agc(d).wait_send()
        ags(d).wait_send()
    for k, d, e in z_sends:
        agz(k, d, e).wait_send()
    exps.wait_send()
    hc_copy.wait_send()

    for q in range(4):
        core_copy(q).wait_send()
        for k in range(6):
            ring(q, k).wait_send()
        for d in range(1, 4):
            direct(q, d).wait_send()

    for b in range(2):

        @pl.loop(1, nz)
        def _(d):
            z_copy(b, d).wait_send()

    @pl.loop(1, nz)
    def _(d):
        zh_copy(d).wait_send()

    for copy in fin_copies:
        copy.wait()
    place = zl * 2 + yl
    for q in range(4):
        block = fin[:, q].reshape(64, 128)
        outt[:, q * 64 : (q + 1) * 64] = block.T
    gw_ref[...] = outt[pl.ds(pl.multiple_of(place * 32, 32), 32), :]
    both = fin[mine, 4] + fin[(1 - yl) * 2 + zl, 4]
    hrow[...] = pltpu.roll(both[0:8], lax.rem(128 - place * 32, 128), 1)
    gg_ref[...] = hrow[pl.ds(zh, 1), 0:32]


def body(tokens, cotangent, weight, gain, exponents):
    width = tokens.shape[1]
    nz = lax.axis_size("rep") // 2
    slab = width // 16
    dma = pltpu.SemaphoreType.DMA
    vmem = pltpu.VMEM
    scratch = [
        vmem((16, 128, slab), BF16),
        vmem((128, 256), BF16),
        vmem((slab, 256), BF16),
        vmem((1, width), BF16),
        vmem((2, width), jnp.int32),
        vmem((2, width), jnp.int32),
        vmem((128, min(slab, 256)), F32),
        vmem((4, 2, 16, 16, slab), BF16),
        vmem((8, 16, 16, slab), BF16),
        vmem((8, 16, 16, slab), BF16),
        vmem((8, 16, 16, slab), BF16),
        vmem((4, 4, 2, 4, 16, slab), BF16),
        vmem((4, 4, 16, slab), BF16),
        vmem((4, 4, 16, slab), BF16),
        vmem((4, 2, 4, 16, slab), BF16),
        vmem((4, 2, 4, 16, slab), BF16),
        vmem((4, 4, 2, 16, slab), BF16),
        vmem((4, 4, 2, 16, slab), BF16),
        vmem((4, 2, 8, 128), F32),
        vmem((4, 2, 8, 128), F32),
        vmem((8, 128), F32),
        vmem((nz, 2, 16, 128), BF16),
        vmem((nz, 2, 16, 128), BF16),
        vmem((nz, 2, 16, 128), BF16),
        vmem((nz, 2, 16, 128), BF16),
        vmem((8, 128), F32),
        vmem((nz, 8, 128), F32),
        vmem((4, 5, 16, 128), F32),
        vmem((128, 256), F32),
        vmem((8, 128), F32),
        pltpu.SemaphoreType.REGULAR((3,)),
        dma((4,)), dma((16,)), dma((4,)), dma((4,)), dma, dma,
        dma((4,)), dma((4,)), dma((2,)), dma((2,)), dma((4,)), dma((4,)), dma((4,)), dma((4,)),
        dma((16,)), dma((16,)),
        dma((24,)), dma((24,)), dma((16,)), dma((16,)), dma((4,)), dma((4,)), dma, dma,
        dma((2 * nz,)), dma((2 * nz,)), dma((nz,)), dma((nz,)), dma((3,)), dma((3,)),
    ]
    any_space = pl.BlockSpec(memory_space=pl.ANY)
    grad_weight, grad_gain = pl.pallas_call(
        functools.partial(kernel, width, slab, nz),
        out_shape=(
            jax.ShapeDtypeStruct((32, 256), F32),
            jax.ShapeDtypeStruct((1, 32), F32),
        ),
        in_specs=[any_space] * 5,
        out_specs=(pl.BlockSpec(memory_space=pltpu.VMEM),) * 2,
        scratch_shapes=scratch,
        compiler_params=pltpu.CompilerParams(
            collective_id=0, has_side_effects=True, vmem_limit_bytes=60 * 2**20
        ),
    )(tokens, cotangent, weight, gain.reshape(1, width), exponents.reshape(2, width))
    return (grad_weight, grad_gain.reshape(32))


def solution(mesh):
    placed = (
        P(("node", "rep"), None),
        P(("node", "rep"), None),
        P("node", None),
        P(),
        P("node", "rep", None, None),
    )
    return jax.shard_map(
        body,
        mesh=mesh,
        in_specs=placed,
        out_specs=(P(("node", "rep"), None), P(("node", "rep"))),
        check_vma=False,
    )
```

```python
import functools

import jax
import jax.numpy as jnp
from jax import lax
from jax.experimental import pallas as pl
from jax.experimental.pallas import tpu as pltpu
from jax.sharding import PartitionSpec as P

EPSILON = 1e-05
SATURATE = 448.0
MESH = pl.DeviceIdType.MESH
F32 = jnp.float32
BF16 = jnp.bfloat16


def device(x, y, z, core):
    return ((x * 2 + lax.div(y, 2)) * 2 + core, z * 2 + lax.rem(y, 2))


def kernel(
    width, slab, nz,
    tok_hbm, cot_hbm, w_hbm, gain_hbm, exp_hbm,
    gw_ref, gg_ref,
    tokv, cotv, wv, gainv, expv, sibexp, invb, wall,
    usend, uown, urecv,
    p1, relp1, relm1, inm1, inp1,
    p2, in2,
    hbuf, hx, hcross, hpair, zxsrc, zxrecv, zown, zsrc0, zsrc1, zrecv0, zrecv1, zhsrc, zhrecv, fin, outt,
    heard, loc_sem, tok_sem, core_s, core_r, exp_s, exp_r,
    agx_s, agx_r, agf_s, agf_r, agc_s, agc_r, ags_s, ags_r, agz_s, agz_r,
    st1_s, st1_r, st2_s, st2_r, hx_s, hx_r, hc_s, hc_r, hz_s, hz_r, zx_s, zx_r, z_s, z_r, zh_s, zh_r, fin_s, fin_r,
):
    node, rep = lax.axis_index("node"), lax.axis_index("rep")
    core = lax.rem(node, 2)
    yh = lax.rem(lax.div(node, 2), 2)
    x = lax.div(node, 4)
    yl = lax.rem(rep, 2)
    z = lax.div(rep, 2)
    y = yh * 2 + yl
    zl, zh = lax.rem(z, 2), lax.div(z, 2)
    zpair = z + 1 - 2 * zl
    ysame = yh * 2 + 1 - yl
    ycross = (1 - yh) * 2 + 1 - yl
    xs = [lax.rem(x + d, 4) for d in range(4)]
    ys = [lax.rem(y + d, 4) for d in range(4)]
    sibling = device(x, y, z, 1 - core)
    tiles = slab // 128

    def remote(src, dst, send, recv, where):
        return pltpu.make_async_remote_copy(
            src_ref=src, dst_ref=dst, send_sem=send, recv_sem=recv, device_id=where, device_id_type=MESH
        )

    loads = [
        pltpu.make_async_copy(w_hbm, wv, loc_sem.at[0]),
        pltpu.make_async_copy(cot_hbm, cotv, loc_sem.at[1]),
        pltpu.make_async_copy(gain_hbm, gainv, loc_sem.at[2]),
        pltpu.make_async_copy(exp_hbm, expv, loc_sem.at[3]),
    ]
    for load in loads:
        load.start()

    def token_load(s):
        at = pl.multiple_of(s * slab, slab)
        return pltpu.make_async_copy(tok_hbm.at[:, pl.ds(at, slab)], tokv.at[s], tok_sem.at[s])

    @pl.loop(0, 16)
    def _(s):
        token_load(s).start()

    barrier = pltpu.get_barrier_semaphore()
    zplus, zminus = lax.rem(z + 1, nz), lax.rem(z + nz - 1, nz)
    partners = [
        sibling,
        device(xs[1], y, z, core), device(xs[2], y, z, core), device(xs[3], y, z, core),
        device(x, ys[1], z, core), device(x, ys[2], z, core), device(x, ys[3], z, core),
        device(x, y, zplus, core), device(x, y, zminus, core),
    ]
    for where in partners:
        pl.semaphore_signal(barrier, inc=1, device_id=where, device_id_type=MESH)

    def tell(k):
        far = 2**k
        listeners = [device(x, y, lax.rem(z + far, nz), core), device(x, y, lax.rem(z + nz - far, nz), core)]
        if k == 0:
            listeners.append(device(x, ysame, z, core))
        if far == 1 or 2 * far < nz:
            for where in listeners:
                pl.semaphore_signal(heard.at[k], inc=1, device_id=where, device_id_type=MESH)

    def hear(k):
        if 2**k == 1 or 2 ** (k + 1) < nz:
            pl.semaphore_wait(heard.at[k], 3 if k == 0 else 2)

    loads[0].wait()
    for t in range(tiles):
        for h in range(2):
            block = wv[t * 128 : (t + 1) * 128, h * 128 : (h + 1) * 128].astype(F32)
            wall[x, yh, h * 8 : (h + 1) * 8, :, t * 128 : (t + 1) * 128] = (
                block.T.astype(BF16).reshape(8, 16, 128)
            )
    loads[1].wait()
    loads[2].wait()
    loads[3].wait()

    xplus, xminus = device(xs[1], y, z, core), device(xs[3], y, z, core)
    yplus, yminus = device(x, ys[1], z, core), device(x, ys[3], z, core)
    cross, same = device(x, ycross, z, core), device(x, ysame, z, core)
    hy = lax.rem(yh + yl, 2)
    first = zl * 8
    yquarter = pl.ds(first + hy * 4, 4)

    def agx(d, k):
        ref = wall.at[x, yh, pl.ds(first + 4 * k, 4)]
        n = d - 1 + k
        return remote(ref, ref, agx_s.at[n], agx_r.at[n], device(xs[d], y, z, core))

    def agf(k):
        ref = wall.at[xs[3 - 2 * k], yh, pl.ds(first + 4 * k, 4)]
        return remote(ref, ref, agf_s.at[k], agf_r.at[k], (xplus, xminus)[k])

    def agc(d):
        ref = wall.at[xs[d], yh, yquarter]
        return remote(ref, ref, agc_s.at[d], agc_r.at[d], cross)

    def ags(d):
        ref = wall.at[xs[d], 1 - yh, yquarter]
        return remote(ref, ref, ags_s.at[d], ags_r.at[d], same)

    def agz(k, d, e):
        ref = wall.at[xs[d], yh if e == 0 else 1 - yh, pl.ds(first + 4 * k, 4)]
        n = k * 8 + e * 4 + d
        there = device(x, y, lax.rem(z + nz + 2 * k - 1, nz), core)
        return remote(ref, ref, agz_s.at[n], agz_r.at[n], there)

    z_sends = [(k, d, e) for k in range(2) for d in range(4) for e in range(2) if d + e]

    def from_x(k):
        agx(1, k).wait_recv()
        agx(3, k).wait_recv()
        agf(k).start()
        agz(k, 3, 0).start()
        agz(k, 1, 0).start()

    def from_opposite():
        for k in range(2):
            agf(k).wait_recv()
            agz(k, 2, 0).start()
        agc(2).start()

    def from_cross(d):
        agc(d).wait_recv()
        ags(d).start()
        agz(hy, d, 1).start()

    def from_same(d):
        ags(d).wait_recv()
        agz(1 - hy, d, 1).start()

    def square(s, total):
        token_load(s).wait()
        for t in range(tiles):
            v = tokv[s, :, t * 128 : (t + 1) * 128].astype(F32)
            total = total + v * v
        return total

    total = lax.fori_loop(0, 16, square, jnp.zeros((128, 128), F32))
    inverse = lax.rsqrt(jnp.sum(total, axis=1, keepdims=True) * (1.0 / width) + EPSILON)
    step = min(slab, 256)
    invb[...] = jnp.broadcast_to(inverse, (128, step))
    cot_t = cotv[...].astype(F32).T.astype(BF16)

    def partial_slab(i, parity, out):
        s = i * 2 + parity
        for t in range(slab // step):
            g = gainv[:, pl.ds(pl.multiple_of(s * slab + t * step, step), step)].astype(F32)
            v = tokv[s, :, t * step : (t + 1) * step].astype(F32)
            normed = (v * invb[...] * g).astype(BF16)
            part = jnp.dot(cot_t, normed, preferred_element_type=F32)
            out[i, :, :, t * step : (t + 1) * step] = part.astype(BF16).reshape(16, 16, step)

    def core_copy(q):
        rows = pl.ds(4 * q, 4)
        return remote(usend.at[:, rows], urecv.at[:, rows], core_s.at[q], core_r.at[q], sibling)

    exps = remote(expv, sibexp, exp_s, exp_r, sibling)

    @pl.loop(0, 8)
    def _(i):
        partial_slab(i, 1 - core, usend)

    pl.semaphore_wait(barrier, len(partners))
    tell(0)
    exps.start()
    core_copy(0).start()
    agx(1, 0).start()
    agx(3, 0).start()
    agx(1, 1).start()
    agx(3, 1).start()
    agc(0).start()
    core_copy(1).start()
    core_copy(2).start()
    core_copy(3).start()

    @pl.loop(0, 8)
    def _(i):
        partial_slab(i, core, uown)

    hear(0)
    tell(1)

    exps.wait_recv()
    parity_at = core * slab

    def threshold(ref, k, i):
        at = pl.multiple_of(i * 2 * slab + parity_at, slab)
        e = ref[k : k + 1, pl.ds(at, slab)]
        return jnp.left_shift(jnp.ones_like(e), e + 30).astype(F32) * (SATURATE * 2.0**-30)

    def combine(q):
        k = q // 2
        core_copy(q).wait_recv()

        @pl.loop(0, 8)
        def _(i):
            px, pyh = lax.div(i, 2), lax.rem(i, 2)
            mine, theirs = threshold(expv, k, i), threshold(sibexp, k, i)
            for lg in range(4):
                a = uown[i, q * 4 + lg].astype(F32)
                b = urecv[i, q * 4 + lg].astype(F32)
                a = jnp.minimum(jnp.maximum(a, -mine), mine)
                b = jnp.minimum(jnp.maximum(b, -theirs), theirs)
                value = (a + b).astype(BF16)
                if q % 2 == 0:
                    p1[q, px, lg // 2, pyh * 2 + lg % 2] = value
                else:
                    p1[q, pyh * 2 + lg // 2, lg % 2, px] = value

    def ring(q, k):
        plus, minus = (xplus, xminus) if q % 2 == 0 else (yplus, yminus)
        at = xs if q % 2 == 0 else ys
        src, dst, where = (
            (p1.at[q, at[2], 0], relp1.at[q], plus),
            (p1.at[q, at[2], 1], relm1.at[q], minus),
            (p1.at[q, at[1], 1], inm1.at[q, 1], plus),
            (p1.at[q, at[3], 0], inp1.at[q, 0], minus),
            (p1.at[q, at[1], 0], inm1.at[q, 0], plus),
            (p1.at[q, at[3], 1], inp1.at[q, 1], minus),
        )[k]
        return remote(src, dst, st1_s.at[q * 6 + k], st1_r.at[q * 6 + k], where)

    def ring_open(q):
        for k in range(4):
            ring(q, k).start()

    def ring_relay(q):
        at = xs if q % 2 == 0 else ys
        for c, d, h, rel in ((0, 1, 0, relp1), (1, 3, 1, relm1)):
            ring(q, c).wait_recv()
            for m in range(4):
                p1[q, at[d], h, m] = (p1[q, at[d], h, m].astype(F32) + rel[q, m].astype(F32)).astype(BF16)
            ring(q, 4 + c).start()

    def direct(q, d):
        there = device(xs[d], y, z, core) if q % 2 == 1 else device(x, ys[d], z, core)
        at = xs if q % 2 == 1 else ys
        n = q * 4 + d
        return remote(p2.at[q, at[d]], in2.at[q, d], st2_s.at[n], st2_r.at[n], there)

    def ring_close(q):
        for k in range(2, 6):
            ring(q, k).wait_recv()
        own = xs[0] if q % 2 == 0 else ys[0]
        for h in range(2):
            for m in range(4):
                value = (
                    p1[q, own, h, m].astype(F32) + inm1[q, h, m].astype(F32) + inp1[q, h, m].astype(F32)
                ).astype(BF16)
                if q % 2 == 0:
                    p2[q, (m // 2) * 2 + h, m % 2] = value
                else:
                    p2[q, m, h] = value
        for d in (2, 1, 3):
            direct(q, d).start()

    def gain_terms():
        @pl.loop(0, 8)
        def _(i):
            px, pyh = lax.div(i, 2), lax.rem(i, 2)
            total = jnp.zeros((16, slab), F32)
            for g in range(16):
                u = uown[i, g].astype(F32) + urecv[i, g].astype(F32)
                total = total + u * wall[px, pyh, g].astype(F32)
            at = pl.multiple_of(i * 2 * slab + parity_at, slab)
            row = jnp.sum(total, axis=0, keepdims=True) / gainv[:, pl.ds(at, slab)].astype(F32)
            if tiles < 8:
                hbuf[px, pyh] = jnp.zeros((8, 128), F32)
            for t in range(tiles):
                hbuf[px, pyh, t : t + 1, :] = row[:, t * 128 : (t + 1) * 128]

    def hx_copy(d):
        return remote(
            hbuf.at[xs[d]], hx.at[d], hx_s.at[d], hx_r.at[d], device(xs[d], y, z, core)
        )

    def pair_copy(q):
        return remote(zxsrc.at[q], zxrecv.at[q], zx_s.at[q], zx_r.at[q], device(x, y, zpair, core))

    def finish(q):
        own = xs[0] if q % 2 == 1 else ys[0]
        for d in (1, 2, 3):
            direct(q, d).wait_recv()

        def value(h):
            return (
                p2[q, own, h].astype(F32) + in2[q, 1, h].astype(F32)
                + in2[q, 2, h].astype(F32) + in2[q, 3, h].astype(F32)
            )

        zxsrc[q] = value(1 - zl).astype(BF16)
        pair_copy(q).start()
        zown[q] = value(zl)

    def pair_finish(q):
        pair_copy(q).wait_recv()
        value = (zown[q] + zxrecv[q].astype(F32)).astype(BF16)
        zsrc = (zsrc0, zsrc1)[q // 2]
        for t in range(tiles):
            zsrc[t, q % 2] = value[:, t * 128 : (t + 1) * 128]

    def z_there(d):
        there = lax.rem(zh + d, tiles)
        return there, device(x, y, there * 2 + zl, core)

    def z_copy(b, d):
        there, where = z_there(d)
        src, dst = ((zsrc0, zrecv0), (zsrc1, zrecv1))[b]
        n = b * tiles + d
        return remote(src.at[there], dst.at[d], z_s.at[n], z_r.at[n], where)

    def zh_copy(d):
        there, where = z_there(d)
        return remote(zhsrc.at[there], zhrecv.at[d], zh_s.at[d], zh_r.at[d], where)

    def z_send(b):
        @pl.loop(1, tiles)
        def _(d):
            z_copy(b, d).start()

    hc_copy = remote(hx.at[0, 1 - yh], hcross, hc_s, hc_r, cross)

    def gain_start():
        for k, d, e in z_sends:
            agz(k, d, e).wait_recv()
        gain_terms()
        for d in range(1, 4):
            hx_copy(d).start()

    def gain_cross():
        for d in range(1, 4):
            hx_copy(d).wait_recv()
        hx[0] = hbuf[x] + hx[1] + hx[2] + hx[3]
        hc_copy.start()

    hz_copy = remote(hpair.at[0], hpair.at[1], hz_s, hz_r, device(x, y, zpair, core))

    def gain_pair():
        hc_copy.wait_recv()
        hpair[0] = hx[0, yh] + hcross[...]
        hz_copy.start()

    def gain_z():
        hz_copy.wait_recv()
        both = hpair[0] + hpair[1]
        for t in range(tiles):
            zhsrc[t] = both[t : t + 1]

        @pl.loop(1, tiles)
        def _(d):
            zh_copy(d).start()

    combine(0)
    ring_open(0)
    combine(1)
    ring_open(1)
    from_x(0)
    from_x(1)
    agc(3).start()
    agc(1).start()
    combine(2)
    combine(3)
    from_cross(0)
    hear(1)
    tell(2)
    ring_relay(0)
    ring_relay(1)
    from_opposite()
    from_cross(3)
    from_cross(1)
    from_same(0)
    ring_close(0)
    ring_close(1)
    ring_open(2)
    ring_open(3)
    from_cross(2)
    from_same(3)
    from_same(1)
    from_same(2)
    ring_relay(2)
    ring_relay(3)
    hear(2)
    finish(0)
    finish(1)
    gain_start()
    pair_finish(0)
    pair_finish(1)
    z_send(0)
    ring_close(2)
    ring_close(3)
    gain_cross()
    finish(2)
    finish(3)
    gain_pair()
    pair_finish(2)
    pair_finish(3)
    z_send(1)
    gain_z()

    mine = yl * 2 + zl
    fin[mine, 0:2] = zsrc0[zh].astype(F32)
    fin[mine, 2:4] = zsrc1[zh].astype(F32)
    fin[mine, 4] = jnp.zeros((16, 128), F32)
    fin[mine, 4, 0:1] = zhsrc[zh]

    for b in range(2):

        @pl.loop(1, tiles)
        def _(d):
            z_copy(b, d).wait_recv()
            if b == 0:
                fin[mine, 0:2] += zrecv0[d].astype(F32)
            else:
                fin[mine, 2:4] += zrecv1[d].astype(F32)

    @pl.loop(1, tiles)
    def _(d):
        zh_copy(d).wait_recv()
        fin[mine, 4, 0:1] += zhrecv[d]

    ends = [device(x, y, zpair, core), device(x, ysame, z, core), device(x, ysame, zpair, core)]
    fin_copies = [
        remote(fin.at[mine], fin.at[mine], fin_s.at[k], fin_r.at[k], ends[k]) for k in range(3)
    ]
    for copy in fin_copies:
        copy.start()

    for d in range(1, 4):
        hx_copy(d).wait_send()
    for k in range(2):
        agx(1, k).wait_send()
        agx(3, k).wait_send()
        agf(k).wait_send()
    for d in range(4):
        agc(d).wait_send()
        ags(d).wait_send()
    for k, d, e in z_sends:
        agz(k, d, e).wait_send()
    exps.wait_send()
    hc_copy.wait_send()

    for q in range(4):
        core_copy(q).wait_send()
        for k in range(6):
            ring(q, k).wait_send()
        for d in range(1, 4):
            direct(q, d).wait_send()

    for q in range(4):
        pair_copy(q).wait_send()
    hz_copy.wait_send()

    for b in range(2):

        @pl.loop(1, tiles)
        def _(d):
            z_copy(b, d).wait_send()

    @pl.loop(1, tiles)
    def _(d):
        zh_copy(d).wait_send()

    for copy in fin_copies:
        copy.wait()
    place = zl * 2 + yl
    for q in range(4):
        block = fin[:, q].reshape(64, 128)
        outt[:, q * 64 : (q + 1) * 64] = block.T
    gw_ref[...] = outt[pl.ds(pl.multiple_of(place * 32, 32), 32), :]
    row = fin[mine, 4, 0:8] + fin[(1 - yl) * 2 + zl, 4, 0:8]
    gg_ref[...] = pltpu.roll(row, lax.rem(128 - place * 32, 128), 1)[0:1, 0:32]


def body(tokens, cotangent, weight, gain, exponents):
    width = tokens.shape[1]
    nz = lax.axis_size("rep") // 2
    slab = width // 16
    dma = pltpu.SemaphoreType.DMA
    vmem = pltpu.VMEM
    scratch = [
        vmem((16, 128, slab), BF16),
        vmem((128, 256), BF16),
        vmem((slab, 256), BF16),
        vmem((1, width), BF16),
        vmem((2, width), jnp.int32),
        vmem((2, width), jnp.int32),
        vmem((128, min(slab, 256)), F32),
        vmem((4, 2, 16, 16, slab), BF16),
        vmem((8, 16, 16, slab), BF16),
        vmem((8, 16, 16, slab), BF16),
        vmem((8, 16, 16, slab), BF16),
        vmem((4, 4, 2, 4, 16, slab), BF16),
        vmem((4, 4, 16, slab), BF16),
        vmem((4, 4, 16, slab), BF16),
        vmem((4, 2, 4, 16, slab), BF16),
        vmem((4, 2, 4, 16, slab), BF16),
        vmem((4, 4, 2, 16, slab), BF16),
        vmem((4, 4, 2, 16, slab), BF16),
        vmem((4, 2, 8, 128), F32),
        vmem((4, 2, 8, 128), F32),
        vmem((8, 128), F32),
        vmem((2, 8, 128), F32),
        vmem((4, 16, slab), BF16),
        vmem((4, 16, slab), BF16),
        vmem((4, 16, slab), F32),
        vmem((slab // 128, 2, 16, 128), BF16),
        vmem((slab // 128, 2, 16, 128), BF16),
        vmem((slab // 128, 2, 16, 128), BF16),
        vmem((slab // 128, 2, 16, 128), BF16),
        vmem((slab // 128, 1, 128), F32),
        vmem((slab // 128, 1, 128), F32),
        vmem((4, 5, 16, 128), F32),
        vmem((128, 256), F32),
        pltpu.SemaphoreType.REGULAR((3,)),
        dma((4,)), dma((16,)), dma((4,)), dma((4,)), dma, dma,
        dma((4,)), dma((4,)), dma((2,)), dma((2,)), dma((4,)), dma((4,)), dma((4,)), dma((4,)),
        dma((16,)), dma((16,)),
        dma((24,)), dma((24,)), dma((16,)), dma((16,)), dma((4,)), dma((4,)), dma, dma,
        dma, dma, dma((4,)), dma((4,)),
        dma((slab // 64,)), dma((slab // 64,)), dma((slab // 128,)), dma((slab // 128,)), dma((3,)), dma((3,)),
    ]
    any_space = pl.BlockSpec(memory_space=pl.ANY)
    grad_weight, grad_gain = pl.pallas_call(
        functools.partial(kernel, width, slab, nz),
        out_shape=(
            jax.ShapeDtypeStruct((32, 256), F32),
            jax.ShapeDtypeStruct((1, 32), F32),
        ),
        in_specs=[any_space] * 5,
        out_specs=(pl.BlockSpec(memory_space=pltpu.VMEM),) * 2,
        scratch_shapes=scratch,
        compiler_params=pltpu.CompilerParams(
            collective_id=0, has_side_effects=True, vmem_limit_bytes=60 * 2**20
        ),
    )(tokens, cotangent, weight, gain.reshape(1, width), exponents.reshape(2, width))
    return (grad_weight, grad_gain.reshape(32))


def solution(mesh):
    placed = (
        P(("node", "rep"), None),
        P(("node", "rep"), None),
        P("node", None),
        P(),
        P("node", "rep", None, None),
    )
    return jax.shard_map(
        body,
        mesh=mesh,
        in_specs=placed,
        out_specs=(P(("node", "rep"), None), P(("node", "rep"))),
        check_vma=False,
    )
```

```python
import functools

import jax
import jax.numpy as jnp
from jax import lax
from jax.experimental import pallas as pl
from jax.experimental.pallas import tpu as pltpu
from jax.sharding import PartitionSpec as P

EPSILON = 1e-05
SATURATE = 448.0
MESH = pl.DeviceIdType.MESH
F32 = jnp.float32
BF16 = jnp.bfloat16


def device(x, y, z, core):
    return ((x * 2 + lax.div(y, 2)) * 2 + core, z * 2 + lax.rem(y, 2))


def kernel(
    width, slab, nz,
    tok_hbm, cot_hbm, w_hbm, gain_hbm, exp_hbm,
    gw_ref, gg_ref,
    tokv, cotv, wv, gainv, expv, sibexp, invb, wall,
    usend, uown, urecv,
    p1, relp1, relm1, inm1, inp1,
    p2, in2,
    hbuf, hx, hcross, hpair, zxsrc, zxrecv, zown, zsrc0, zsrc1, zrecv0, zrecv1, zhsrc, zhrecv, fin, outt,
    heard, loc_sem, tok_sem, core_s, core_r, exp_s, exp_r,
    agx_s, agx_r, agf_s, agf_r, agc_s, agc_r, ags_s, ags_r, agz_s, agz_r,
    st1_s, st1_r, st2_s, st2_r, hx_s, hx_r, hc_s, hc_r, hz_s, hz_r, zx_s, zx_r, z_s, z_r, zh_s, zh_r, fin_s, fin_r,
):
    node, rep = lax.axis_index("node"), lax.axis_index("rep")
    core = lax.rem(node, 2)
    yh = lax.rem(lax.div(node, 2), 2)
    x = lax.div(node, 4)
    yl = lax.rem(rep, 2)
    z = lax.div(rep, 2)
    y = yh * 2 + yl
    zl, zh = lax.rem(z, 2), lax.div(z, 2)
    zpair = z + 1 - 2 * zl
    ysame = yh * 2 + 1 - yl
    ycross = (1 - yh) * 2 + 1 - yl
    xs = [lax.rem(x + d, 4) for d in range(4)]
    ys = [lax.rem(y + d, 4) for d in range(4)]
    sibling = device(x, y, z, 1 - core)
    tiles = slab // 128

    def remote(src, dst, send, recv, where):
        return pltpu.make_async_remote_copy(
            src_ref=src, dst_ref=dst, send_sem=send, recv_sem=recv, device_id=where, device_id_type=MESH
        )

    loads = [
        pltpu.make_async_copy(w_hbm, wv, loc_sem.at[0]),
        pltpu.make_async_copy(cot_hbm, cotv, loc_sem.at[1]),
        pltpu.make_async_copy(gain_hbm, gainv, loc_sem.at[2]),
        pltpu.make_async_copy(exp_hbm, expv, loc_sem.at[3]),
    ]
    for load in loads:
        load.start()

    def token_load(s):
        at = pl.multiple_of(s * slab, slab)
        return pltpu.make_async_copy(tok_hbm.at[:, pl.ds(at, slab)], tokv.at[s], tok_sem.at[s])

    @pl.loop(0, 16)
    def _(s):
        token_load(s).start()

    barrier = pltpu.get_barrier_semaphore()
    zplus, zminus = lax.rem(z + 1, nz), lax.rem(z + nz - 1, nz)
    partners = [
        sibling,
        device(xs[1], y, z, core), device(xs[2], y, z, core), device(xs[3], y, z, core),
        device(x, ys[1], z, core), device(x, ys[2], z, core), device(x, ys[3], z, core),
        device(x, y, zplus, core), device(x, y, zminus, core),
    ]
    for where in partners:
        pl.semaphore_signal(barrier, inc=1, device_id=where, device_id_type=MESH)

    def tell(k):
        far = 2**k
        listeners = [device(x, y, lax.rem(z + far, nz), core), device(x, y, lax.rem(z + nz - far, nz), core)]
        if k == 0:
            listeners.append(device(x, ysame, z, core))
        if far == 1 or 2 * far < nz:
            for where in listeners:
                pl.semaphore_signal(heard.at[k], inc=1, device_id=where, device_id_type=MESH)

    def hear(k):
        if 2**k == 1 or 2 ** (k + 1) < nz:
            pl.semaphore_wait(heard.at[k], 3 if k == 0 else 2)

    loads[0].wait()
    for t in range(tiles):
        for h in range(2):
            block = wv[t * 128 : (t + 1) * 128, h * 128 : (h + 1) * 128].astype(F32)
            wall[x, yh, h * 8 : (h + 1) * 8, :, t * 128 : (t + 1) * 128] = (
                block.T.astype(BF16).reshape(8, 16, 128)
            )
    loads[1].wait()
    loads[2].wait()
    loads[3].wait()

    xplus, xminus = device(xs[1], y, z, core), device(xs[3], y, z, core)
    yplus, yminus = device(x, ys[1], z, core), device(x, ys[3], z, core)
    cross, same = device(x, ycross, z, core), device(x, ysame, z, core)
    hy = lax.rem(yh + yl, 2)
    first = zl * 8
    yquarter = pl.ds(first + hy * 4, 4)

    def agx(d, k):
        ref = wall.at[x, yh, pl.ds(first + 4 * k, 4)]
        n = d - 1 + k
        return remote(ref, ref, agx_s.at[n], agx_r.at[n], device(xs[d], y, z, core))

    def agf(k):
        ref = wall.at[xs[3 - 2 * k], yh, pl.ds(first + 4 * k, 4)]
        return remote(ref, ref, agf_s.at[k], agf_r.at[k], (xplus, xminus)[k])

    def agc(d):
        ref = wall.at[xs[d], yh, yquarter]
        return remote(ref, ref, agc_s.at[d], agc_r.at[d], cross)

    def ags(d):
        ref = wall.at[xs[d], 1 - yh, yquarter]
        return remote(ref, ref, ags_s.at[d], ags_r.at[d], same)

    def agz(k, d, e):
        ref = wall.at[xs[d], yh if e == 0 else 1 - yh, pl.ds(first + 4 * k, 4)]
        n = k * 8 + e * 4 + d
        there = device(x, y, lax.rem(z + nz + 2 * k - 1, nz), core)
        return remote(ref, ref, agz_s.at[n], agz_r.at[n], there)

    z_sends = [(k, d, e) for k in range(2) for d in range(4) for e in range(2) if d + e]

    def from_x(k):
        agx(1, k).wait_recv()
        agx(3, k).wait_recv()
        agf(k).start()
        agz(k, 3, 0).start()
        agz(k, 1, 0).start()

    def from_opposite():
        for k in range(2):
            agf(k).wait_recv()
            agz(k, 2, 0).start()
        agc(2).start()

    def from_cross(d):
        agc(d).wait_recv()
        ags(d).start()
        agz(hy, d, 1).start()

    def from_same(d):
        ags(d).wait_recv()
        agz(1 - hy, d, 1).start()

    def square(s, total):
        token_load(s).wait()
        for t in range(tiles):
            v = tokv[s, :, t * 128 : (t + 1) * 128].astype(F32)
            total = total + v * v
        return total

    total = lax.fori_loop(0, 16, square, jnp.zeros((128, 128), F32))
    inverse = lax.rsqrt(jnp.sum(total, axis=1, keepdims=True) * (1.0 / width) + EPSILON)
    step = min(slab, 256)
    invb[...] = jnp.broadcast_to(inverse, (128, step))
    cot_t = cotv[...].astype(F32).T.astype(BF16)

    def gain_row(at, size):
        return gainv[pl.ds(pl.multiple_of(at, size), size)].astype(F32).reshape(1, size)

    def partial_slab(i, parity, out):
        s = i * 2 + parity
        for t in range(slab // step):
            g = gain_row(s * slab + t * step, step)
            v = tokv[s, :, t * step : (t + 1) * step].astype(F32)
            normed = (v * invb[...] * g).astype(BF16)
            part = jnp.dot(cot_t, normed, preferred_element_type=F32)
            out[i, :, :, t * step : (t + 1) * step] = part.astype(BF16).reshape(16, 16, step)

    def core_copy(q):
        rows = pl.ds(4 * q, 4)
        return remote(usend.at[:, rows], urecv.at[:, rows], core_s.at[q], core_r.at[q], sibling)

    exps = remote(expv, sibexp, exp_s, exp_r, sibling)

    @pl.loop(0, 2)
    def _(i):
        partial_slab(i * 4, 1 - core, usend)
        partial_slab(i * 4 + 1, 1 - core, usend)
        partial_slab(i * 4 + 2, 1 - core, usend)
        partial_slab(i * 4 + 3, 1 - core, usend)

    pl.semaphore_wait(barrier, len(partners))
    tell(0)
    exps.start()
    core_copy(0).start()
    agx(1, 0).start()
    agx(3, 0).start()
    agx(1, 1).start()
    agx(3, 1).start()
    agc(0).start()
    core_copy(1).start()
    core_copy(2).start()
    core_copy(3).start()

    @pl.loop(0, 2)
    def _(i):
        partial_slab(i * 4, core, uown)
        partial_slab(i * 4 + 1, core, uown)
        partial_slab(i * 4 + 2, core, uown)
        partial_slab(i * 4 + 3, core, uown)

    hear(0)
    tell(1)

    exps.wait_recv()
    parity_at = core * slab

    def threshold(ref, k, i):
        at = pl.multiple_of(i * 2 * slab + parity_at, slab)
        e = ref[k : k + 1, pl.ds(at, slab)]
        return jnp.left_shift(jnp.ones_like(e), e + 30).astype(F32) * (SATURATE * 2.0**-30)

    def combine(q):
        k = q // 2
        core_copy(q).wait_recv()

        @pl.loop(0, 8)
        def _(i):
            px, pyh = lax.div(i, 2), lax.rem(i, 2)
            mine, theirs = threshold(expv, k, i), threshold(sibexp, k, i)
            for lg in range(4):
                a = uown[i, q * 4 + lg].astype(F32)
                b = urecv[i, q * 4 + lg].astype(F32)
                a = jnp.minimum(jnp.maximum(a, -mine), mine)
                b = jnp.minimum(jnp.maximum(b, -theirs), theirs)
                value = (a + b).astype(BF16)
                if q % 2 == 0:
                    p1[q, px, lg // 2, pyh * 2 + lg % 2] = value
                else:
                    p1[q, pyh * 2 + lg // 2, lg % 2, px] = value

    def ring(q, k):
        plus, minus = (xplus, xminus) if q % 2 == 0 else (yplus, yminus)
        at = xs if q % 2 == 0 else ys
        src, dst, where = (
            (p1.at[q, at[2], 0], relp1.at[q], plus),
            (p1.at[q, at[2], 1], relm1.at[q], minus),
            (p1.at[q, at[1], 1], inm1.at[q, 1], plus),
            (p1.at[q, at[3], 0], inp1.at[q, 0], minus),
            (p1.at[q, at[1], 0], inm1.at[q, 0], plus),
            (p1.at[q, at[3], 1], inp1.at[q, 1], minus),
        )[k]
        return remote(src, dst, st1_s.at[q * 6 + k], st1_r.at[q * 6 + k], where)

    def ring_open(q):
        for k in range(4):
            ring(q, k).start()

    def ring_relay(q):
        at = xs if q % 2 == 0 else ys
        for c, d, h, rel in ((0, 1, 0, relp1), (1, 3, 1, relm1)):
            ring(q, c).wait_recv()
            for m in range(4):
                p1[q, at[d], h, m] = (p1[q, at[d], h, m].astype(F32) + rel[q, m].astype(F32)).astype(BF16)
            ring(q, 4 + c).start()

    def direct(q, d):
        there = device(xs[d], y, z, core) if q % 2 == 1 else device(x, ys[d], z, core)
        at = xs if q % 2 == 1 else ys
        n = q * 4 + d
        return remote(p2.at[q, at[d]], in2.at[q, d], st2_s.at[n], st2_r.at[n], there)

    def ring_close(q):
        for k in range(2, 6):
            ring(q, k).wait_recv()
        own = xs[0] if q % 2 == 0 else ys[0]
        for h in range(2):
            for m in range(4):
                value = (
                    p1[q, own, h, m].astype(F32) + inm1[q, h, m].astype(F32) + inp1[q, h, m].astype(F32)
                ).astype(BF16)
                if q % 2 == 0:
                    p2[q, (m // 2) * 2 + h, m % 2] = value
                else:
                    p2[q, m, h] = value
        for d in (2, 1, 3):
            direct(q, d).start()

    def gain_terms():
        @pl.loop(0, 8)
        def _(i):
            px, pyh = lax.div(i, 2), lax.rem(i, 2)
            total = jnp.zeros((16, slab), F32)
            for g in range(16):
                u = uown[i, g].astype(F32) + urecv[i, g].astype(F32)
                total = total + u * wall[px, pyh, g].astype(F32)
            at = pl.multiple_of(i * 2 * slab + parity_at, slab)
            row = jnp.sum(total, axis=0, keepdims=True) / gain_row(at, slab)
            if tiles < 8:
                hbuf[px, pyh] = jnp.zeros((8, 128), F32)
            for t in range(tiles):
                hbuf[px, pyh, t : t + 1, :] = row[:, t * 128 : (t + 1) * 128]

    def hx_copy(d):
        return remote(
            hbuf.at[xs[d]], hx.at[d], hx_s.at[d], hx_r.at[d], device(xs[d], y, z, core)
        )

    def pair_copy(q):
        return remote(zxsrc.at[q], zxrecv.at[q], zx_s.at[q], zx_r.at[q], device(x, y, zpair, core))

    def finish(q):
        own = xs[0] if q % 2 == 1 else ys[0]
        for d in (1, 2, 3):
            direct(q, d).wait_recv()

        def value(h):
            return (
                p2[q, own, h].astype(F32) + in2[q, 1, h].astype(F32)
                + in2[q, 2, h].astype(F32) + in2[q, 3, h].astype(F32)
            )

        zxsrc[q] = value(1 - zl).astype(BF16)
        pair_copy(q).start()
        zown[q] = value(zl)

    def pair_finish(q):
        pair_copy(q).wait_recv()
        value = (zown[q] + zxrecv[q].astype(F32)).astype(BF16)
        zsrc = (zsrc0, zsrc1)[q // 2]
        for t in range(tiles):
            zsrc[t, q % 2] = value[:, t * 128 : (t + 1) * 128]

    def z_there(d):
        there = lax.rem(zh + d, tiles)
        return there, device(x, y, there * 2 + zl, core)

    def z_copy(b, d):
        there, where = z_there(d)
        src, dst = ((zsrc0, zrecv0), (zsrc1, zrecv1))[b]
        n = b * tiles + d
        return remote(src.at[there], dst.at[d], z_s.at[n], z_r.at[n], where)

    def zh_copy(d):
        there, where = z_there(d)
        return remote(zhsrc.at[there], zhrecv.at[d], zh_s.at[d], zh_r.at[d], where)

    def z_send(b):
        @pl.loop(1, tiles)
        def _(d):
            z_copy(b, d).start()

    hc_copy = remote(hx.at[0, 1 - yh], hcross, hc_s, hc_r, cross)

    def gain_start():
        for k, d, e in z_sends:
            agz(k, d, e).wait_recv()
        gain_terms()
        for d in range(1, 4):
            hx_copy(d).start()

    def gain_cross():
        for d in range(1, 4):
            hx_copy(d).wait_recv()
        hx[0] = hbuf[x] + hx[1] + hx[2] + hx[3]
        hc_copy.start()

    hz_copy = remote(hpair.at[0], hpair.at[1], hz_s, hz_r, device(x, y, zpair, core))

    def gain_pair():
        hc_copy.wait_recv()
        hpair[0] = hx[0, yh] + hcross[...]
        hz_copy.start()

    def gain_z():
        hz_copy.wait_recv()
        both = hpair[0] + hpair[1]
        for t in range(tiles):
            zhsrc[t] = both[t : t + 1]

        @pl.loop(1, tiles)
        def _(d):
            zh_copy(d).start()

    combine(0)
    ring_open(0)
    combine(1)
    ring_open(1)
    from_x(0)
    from_x(1)
    agc(3).start()
    agc(1).start()
    combine(2)
    combine(3)
    from_cross(0)
    hear(1)
    tell(2)
    ring_relay(0)
    ring_relay(1)
    from_opposite()
    from_cross(3)
    from_cross(1)
    from_same(0)
    ring_close(0)
    ring_close(1)
    ring_open(2)
    ring_open(3)
    from_cross(2)
    from_same(3)
    from_same(1)
    from_same(2)
    ring_relay(2)
    ring_relay(3)
    hear(2)
    finish(0)
    finish(1)
    gain_start()
    pair_finish(0)
    pair_finish(1)
    z_send(0)
    ring_close(2)
    ring_close(3)
    gain_cross()
    finish(2)
    finish(3)
    gain_pair()
    pair_finish(2)
    pair_finish(3)
    z_send(1)
    gain_z()

    mine = yl * 2 + zl
    fin[mine, 0:2] = zsrc0[zh].astype(F32)
    fin[mine, 2:4] = zsrc1[zh].astype(F32)
    fin[mine, 4] = jnp.zeros((16, 128), F32)
    fin[mine, 4, 0:1] = zhsrc[zh]

    for b in range(2):

        @pl.loop(1, tiles)
        def _(d):
            z_copy(b, d).wait_recv()
            if b == 0:
                fin[mine, 0:2] += zrecv0[d].astype(F32)
            else:
                fin[mine, 2:4] += zrecv1[d].astype(F32)

    @pl.loop(1, tiles)
    def _(d):
        zh_copy(d).wait_recv()
        fin[mine, 4, 0:1] += zhrecv[d]

    ends = [device(x, y, zpair, core), device(x, ysame, z, core), device(x, ysame, zpair, core)]
    fin_copies = [
        remote(fin.at[mine], fin.at[mine], fin_s.at[k], fin_r.at[k], ends[k]) for k in range(3)
    ]
    for copy in fin_copies:
        copy.start()

    for d in range(1, 4):
        hx_copy(d).wait_send()
    for k in range(2):
        agx(1, k).wait_send()
        agx(3, k).wait_send()
        agf(k).wait_send()
    for d in range(4):
        agc(d).wait_send()
        ags(d).wait_send()
    for k, d, e in z_sends:
        agz(k, d, e).wait_send()
    exps.wait_send()
    hc_copy.wait_send()

    for q in range(4):
        core_copy(q).wait_send()
        for k in range(6):
            ring(q, k).wait_send()
        for d in range(1, 4):
            direct(q, d).wait_send()

    for q in range(4):
        pair_copy(q).wait_send()
    hz_copy.wait_send()

    for b in range(2):

        @pl.loop(1, tiles)
        def _(d):
            z_copy(b, d).wait_send()

    @pl.loop(1, tiles)
    def _(d):
        zh_copy(d).wait_send()

    for copy in fin_copies:
        copy.wait()
    place = zl * 2 + yl
    for q in range(4):
        block = fin[:, q].reshape(64, 128)
        outt[:, q * 64 : (q + 1) * 64] = block.T
    gw_ref[...] = outt[pl.ds(pl.multiple_of(place * 32, 32), 32), :]
    row = fin[mine, 4, 0:8] + fin[(1 - yl) * 2 + zl, 4, 0:8]
    gg_ref[...] = pltpu.roll(row, lax.rem(128 - place * 32, 128), 1)[0:1, 0:32]


def hand_over(gw_ref, gg_ref, gw_out, gg_out, sem):
    copies = [
        pltpu.make_async_copy(gw_ref, gw_out, sem.at[0]),
        pltpu.make_async_copy(gg_ref, gg_out, sem.at[1]),
    ]
    for copy in copies:
        copy.start()
    for copy in copies:
        copy.wait()


def body(tokens, cotangent, weight, gain, exponents):
    width = tokens.shape[1]
    nz = lax.axis_size("rep") // 2
    slab = width // 16
    dma = pltpu.SemaphoreType.DMA
    vmem = pltpu.VMEM
    scratch = [
        vmem((16, 128, slab), BF16),
        vmem((128, 256), BF16),
        vmem((slab, 256), BF16),
        vmem((width,), BF16),
        vmem((2, width), jnp.int32),
        vmem((2, width), jnp.int32),
        vmem((128, min(slab, 256)), F32),
        vmem((4, 2, 16, 16, slab), BF16),
        vmem((8, 16, 16, slab), BF16),
        vmem((8, 16, 16, slab), BF16),
        vmem((8, 16, 16, slab), BF16),
        vmem((4, 4, 2, 4, 16, slab), BF16),
        vmem((4, 4, 16, slab), BF16),
        vmem((4, 4, 16, slab), BF16),
        vmem((4, 2, 4, 16, slab), BF16),
        vmem((4, 2, 4, 16, slab), BF16),
        vmem((4, 4, 2, 16, slab), BF16),
        vmem((4, 4, 2, 16, slab), BF16),
        vmem((4, 2, 8, 128), F32),
        vmem((4, 2, 8, 128), F32),
        vmem((8, 128), F32),
        vmem((2, 8, 128), F32),
        vmem((4, 16, slab), BF16),
        vmem((4, 16, slab), BF16),
        vmem((4, 16, slab), F32),
        vmem((slab // 128, 2, 16, 128), BF16),
        vmem((slab // 128, 2, 16, 128), BF16),
        vmem((slab // 128, 2, 16, 128), BF16),
        vmem((slab // 128, 2, 16, 128), BF16),
        vmem((slab // 128, 1, 128), F32),
        vmem((slab // 128, 1, 128), F32),
        vmem((4, 5, 16, 128), F32),
        vmem((128, 256), F32),
        pltpu.SemaphoreType.REGULAR((3,)),
        dma((4,)), dma((16,)), dma((4,)), dma((4,)), dma, dma,
        dma((4,)), dma((4,)), dma((2,)), dma((2,)), dma((4,)), dma((4,)), dma((4,)), dma((4,)),
        dma((16,)), dma((16,)),
        dma((24,)), dma((24,)), dma((16,)), dma((16,)), dma((4,)), dma((4,)), dma, dma,
        dma, dma, dma((4,)), dma((4,)),
        dma((slab // 64,)), dma((slab // 64,)), dma((slab // 128,)), dma((slab // 128,)), dma((3,)), dma((3,)),
    ]
    any_space = pl.BlockSpec(memory_space=pl.ANY)
    grad_weight, grad_gain = pl.pallas_call(
        functools.partial(kernel, width, slab, nz),
        out_shape=(
            jax.ShapeDtypeStruct((32, 256), F32),
            jax.ShapeDtypeStruct((1, 32), F32),
        ),
        in_specs=[any_space] * 5,
        out_specs=(pl.BlockSpec(memory_space=pltpu.VMEM),) * 2,
        scratch_shapes=scratch,
        compiler_params=pltpu.CompilerParams(
            collective_id=0, has_side_effects=True, vmem_limit_bytes=60 * 2**20
        ),
    )(tokens, cotangent, weight, gain, exponents.reshape(2, width))
    grad_weight, grad_gain = pl.pallas_call(
        hand_over,
        out_shape=(
            jax.ShapeDtypeStruct((32, 256), F32),
            jax.ShapeDtypeStruct((1, 32), F32),
        ),
        in_specs=[any_space] * 2,
        out_specs=(any_space,) * 2,
        scratch_shapes=[dma((2,))],
        compiler_params=pltpu.CompilerParams(vmem_limit_bytes=60 * 2**20),
    )(grad_weight, grad_gain)
    return (grad_weight, grad_gain.reshape(32))


def solution(mesh):
    placed = (
        P(("node", "rep"), None),
        P(("node", "rep"), None),
        P("node", None),
        P(),
        P("node", "rep", None, None),
    )
    return jax.shard_map(
        body,
        mesh=mesh,
        in_specs=placed,
        out_specs=(P(("node", "rep"), None), P(("node", "rep"))),
        check_vma=False,
    )
```

```python
import functools

import jax
import jax.numpy as jnp
from jax import lax
from jax.experimental import pallas as pl
from jax.experimental.pallas import tpu as pltpu
from jax.sharding import PartitionSpec as P

EPSILON = 1e-05
SATURATE = 448.0
MESH = pl.DeviceIdType.MESH
F32 = jnp.float32
BF16 = jnp.bfloat16


def device(x, y, z, core):
    return ((x * 2 + lax.div(y, 2)) * 2 + core, z * 2 + lax.rem(y, 2))


def kernel(
    width, slab, nz,
    tok_hbm, cot_hbm, w_hbm, gain_hbm, exp_hbm,
    gw_ref, gg_ref,
    tokv, cotv, wv, gainv, expv, sibexp, invb, wall,
    usend, uown, urecv,
    p1, relp1, relm1, inm1, inp1,
    p2, in2,
    hbuf, hx, hcross, hpair, zxsrc, zxrecv, zown, zsrc0, zsrc1, zrecv0, zrecv1, zhsrc, zhrecv, fin, outt,
    heard, loc_sem, tok_sem, core_s, core_r, exp_s, exp_r,
    agx_s, agx_r, agf_s, agf_r, agc_s, agc_r, ags_s, ags_r, agz_s, agz_r,
    st1_s, st1_r, st2_s, st2_r, hx_s, hx_r, hc_s, hc_r, hz_s, hz_r, zx_s, zx_r, z_s, z_r, zh_s, zh_r, fin_s, fin_r,
):
    node, rep = lax.axis_index("node"), lax.axis_index("rep")
    core = lax.rem(node, 2)
    yh = lax.rem(lax.div(node, 2), 2)
    x = lax.div(node, 4)
    yl = lax.rem(rep, 2)
    z = lax.div(rep, 2)
    y = yh * 2 + yl
    zl, zh = lax.rem(z, 2), lax.div(z, 2)
    zpair = z + 1 - 2 * zl
    ysame = yh * 2 + 1 - yl
    ycross = (1 - yh) * 2 + 1 - yl
    xs = [lax.rem(x + d, 4) for d in range(4)]
    ys = [lax.rem(y + d, 4) for d in range(4)]
    sibling = device(x, y, z, 1 - core)
    tiles = slab // 128

    def remote(src, dst, send, recv, where):
        return pltpu.make_async_remote_copy(
            src_ref=src, dst_ref=dst, send_sem=send, recv_sem=recv, device_id=where, device_id_type=MESH
        )

    loads = [
        pltpu.make_async_copy(w_hbm, wv, loc_sem.at[0]),
        pltpu.make_async_copy(cot_hbm, cotv, loc_sem.at[1]),
        pltpu.make_async_copy(gain_hbm, gainv, loc_sem.at[2]),
        pltpu.make_async_copy(exp_hbm, expv, loc_sem.at[3]),
    ]
    for load in loads:
        load.start()

    def token_load(s):
        at = pl.multiple_of(s * slab, slab)
        return pltpu.make_async_copy(tok_hbm.at[:, pl.ds(at, slab)], tokv.at[s], tok_sem.at[s])

    @pl.loop(0, 16)
    def _(s):
        token_load(s).start()

    barrier = pltpu.get_barrier_semaphore()
    zplus, zminus = lax.rem(z + 1, nz), lax.rem(z + nz - 1, nz)
    partners = [
        sibling,
        device(xs[1], y, z, core), device(xs[2], y, z, core), device(xs[3], y, z, core),
        device(x, ys[1], z, core), device(x, ys[2], z, core), device(x, ys[3], z, core),
        device(x, y, zplus, core), device(x, y, zminus, core),
    ]
    for where in partners:
        pl.semaphore_signal(barrier, inc=1, device_id=where, device_id_type=MESH)

    def tell(k):
        far = 2**k
        listeners = [device(x, y, lax.rem(z + far, nz), core), device(x, y, lax.rem(z + nz - far, nz), core)]
        if k == 0:
            listeners.append(device(x, ysame, z, core))
        if far == 1 or 2 * far < nz:
            for where in listeners:
                pl.semaphore_signal(heard.at[k], inc=1, device_id=where, device_id_type=MESH)

    def hear(k):
        if 2**k == 1 or 2 ** (k + 1) < nz:
            pl.semaphore_wait(heard.at[k], 3 if k == 0 else 2)

    loads[0].wait()
    for t in range(tiles):
        for h in range(2):
            block = wv[t * 128 : (t + 1) * 128, h * 128 : (h + 1) * 128].astype(F32)
            wall[x, yh, h * 8 : (h + 1) * 8, :, t * 128 : (t + 1) * 128] = (
                block.T.astype(BF16).reshape(8, 16, 128)
            )
    loads[1].wait()
    loads[2].wait()
    loads[3].wait()

    xplus, xminus = device(xs[1], y, z, core), device(xs[3], y, z, core)
    yplus, yminus = device(x, ys[1], z, core), device(x, ys[3], z, core)
    cross, same = device(x, ycross, z, core), device(x, ysame, z, core)
    hy = lax.rem(yh + yl, 2)
    first = zl * 8
    yquarter = pl.ds(first + hy * 4, 4)

    def agx(d, k):
        ref = wall.at[x, yh, pl.ds(first + 4 * k, 4)]
        n = d - 1 + k
        return remote(ref, ref, agx_s.at[n], agx_r.at[n], device(xs[d], y, z, core))

    def agf(k):
        ref = wall.at[xs[3 - 2 * k], yh, pl.ds(first + 4 * k, 4)]
        return remote(ref, ref, agf_s.at[k], agf_r.at[k], (xplus, xminus)[k])

    def agc(d):
        ref = wall.at[xs[d], yh, yquarter]
        return remote(ref, ref, agc_s.at[d], agc_r.at[d], cross)

    def ags(d):
        ref = wall.at[xs[d], 1 - yh, yquarter]
        return remote(ref, ref, ags_s.at[d], ags_r.at[d], same)

    def agz(k, d, e):
        ref = wall.at[xs[d], yh if e == 0 else 1 - yh, pl.ds(first + 4 * k, 4)]
        n = k * 8 + e * 4 + d
        there = device(x, y, lax.rem(z + nz + 2 * k - 1, nz), core)
        return remote(ref, ref, agz_s.at[n], agz_r.at[n], there)

    z_sends = [(k, d, e) for k in range(2) for d in range(4) for e in range(2) if d + e]

    def from_x(k):
        agx(1, k).wait_recv()
        agx(3, k).wait_recv()
        agf(k).start()
        agz(k, 3, 0).start()
        agz(k, 1, 0).start()

    def from_opposite():
        for k in range(2):
            agf(k).wait_recv()
            agz(k, 2, 0).start()
        agc(2).start()

    def from_cross(d):
        agc(d).wait_recv()
        ags(d).start()
        agz(hy, d, 1).start()

    def from_same(d):
        ags(d).wait_recv()
        agz(1 - hy, d, 1).start()

    def square(s, total):
        token_load(s).wait()
        for t in range(tiles):
            v = tokv[s, :, t * 128 : (t + 1) * 128].astype(F32)
            total = total + v * v
        return total

    total = lax.fori_loop(0, 16, square, jnp.zeros((128, 128), F32))
    inverse = lax.rsqrt(jnp.sum(total, axis=1, keepdims=True) * (1.0 / width) + EPSILON)
    step = min(slab, 256)
    invb[...] = jnp.broadcast_to(inverse, (128, step))
    cot_t = cotv[...].astype(F32).T.astype(BF16)

    def gain_row(at, size):
        return gainv[pl.ds(pl.multiple_of(at, size), size)].astype(F32).reshape(1, size)

    def partial_slab(i, parity, out):
        s = i * 2 + parity
        for t in range(slab // step):
            g = gain_row(s * slab + t * step, step)
            v = tokv[s, :, t * step : (t + 1) * step].astype(F32)
            normed = (v * invb[...] * g).astype(BF16)
            part = jnp.dot(cot_t, normed, preferred_element_type=F32)
            out[i, :, :, t * step : (t + 1) * step] = part.astype(BF16).reshape(16, 16, step)

    def core_copy(q):
        rows = pl.ds(4 * q, 4)
        return remote(usend.at[:, rows], urecv.at[:, rows], core_s.at[q], core_r.at[q], sibling)

    exps = remote(expv, sibexp, exp_s, exp_r, sibling)

    @pl.loop(0, 2)
    def _(i):
        partial_slab(i * 4, 1 - core, usend)
        partial_slab(i * 4 + 1, 1 - core, usend)
        partial_slab(i * 4 + 2, 1 - core, usend)
        partial_slab(i * 4 + 3, 1 - core, usend)

    pl.semaphore_wait(barrier, len(partners))
    tell(0)
    exps.start()
    core_copy(0).start()
    agx(1, 0).start()
    agx(3, 0).start()
    agx(1, 1).start()
    agx(3, 1).start()
    agc(0).start()
    core_copy(1).start()
    core_copy(2).start()
    core_copy(3).start()

    @pl.loop(0, 2)
    def _(i):
        partial_slab(i * 4, core, uown)
        partial_slab(i * 4 + 1, core, uown)
        partial_slab(i * 4 + 2, core, uown)
        partial_slab(i * 4 + 3, core, uown)

    hear(0)
    tell(1)

    exps.wait_recv()
    parity_at = core * slab

    def threshold(ref, k, i):
        at = pl.multiple_of(i * 2 * slab + parity_at, slab)
        e = ref[k : k + 1, pl.ds(at, slab)]
        return jnp.left_shift(jnp.ones_like(e), e + 30).astype(F32) * (SATURATE * 2.0**-30)

    def combine(q):
        k = q // 2
        core_copy(q).wait_recv()

        @pl.loop(0, 8)
        def _(i):
            px, pyh = lax.div(i, 2), lax.rem(i, 2)
            mine, theirs = threshold(expv, k, i), threshold(sibexp, k, i)
            for lg in range(4):
                a = uown[i, q * 4 + lg].astype(F32)
                b = urecv[i, q * 4 + lg].astype(F32)
                a = jnp.minimum(jnp.maximum(a, -mine), mine)
                b = jnp.minimum(jnp.maximum(b, -theirs), theirs)
                value = (a + b).astype(BF16)
                if q % 2 == 0:
                    p1[q, px, lg // 2, pyh * 2 + lg % 2] = value
                else:
                    p1[q, pyh * 2 + lg // 2, lg % 2, px] = value

    def ring(q, k):
        plus, minus = (xplus, xminus) if q % 2 == 0 else (yplus, yminus)
        at = xs if q % 2 == 0 else ys
        src, dst, where = (
            (p1.at[q, at[2], 0], relp1.at[q], plus),
            (p1.at[q, at[2], 1], relm1.at[q], minus),
            (p1.at[q, at[1], 1], inm1.at[q, 1], plus),
            (p1.at[q, at[3], 0], inp1.at[q, 0], minus),
            (p1.at[q, at[1], 0], inm1.at[q, 0], plus),
            (p1.at[q, at[3], 1], inp1.at[q, 1], minus),
        )[k]
        return remote(src, dst, st1_s.at[q * 6 + k], st1_r.at[q * 6 + k], where)

    def ring_open(q):
        for k in range(4):
            ring(q, k).start()

    def ring_relay(q):
        at = xs if q % 2 == 0 else ys
        for c, d, h, rel in ((0, 1, 0, relp1), (1, 3, 1, relm1)):
            ring(q, c).wait_recv()
            for m in range(4):
                p1[q, at[d], h, m] = (p1[q, at[d], h, m].astype(F32) + rel[q, m].astype(F32)).astype(BF16)
            ring(q, 4 + c).start()

    def direct(q, d):
        there = device(xs[d], y, z, core) if q % 2 == 1 else device(x, ys[d], z, core)
        at = xs if q % 2 == 1 else ys
        n = q * 4 + d
        return remote(p2.at[q, at[d]], in2.at[q, d], st2_s.at[n], st2_r.at[n], there)

    def ring_close(q):
        for k in range(2, 6):
            ring(q, k).wait_recv()
        own = xs[0] if q % 2 == 0 else ys[0]
        for h in range(2):
            for m in range(4):
                value = (
                    p1[q, own, h, m].astype(F32) + inm1[q, h, m].astype(F32) + inp1[q, h, m].astype(F32)
                ).astype(BF16)
                if q % 2 == 0:
                    p2[q, (m // 2) * 2 + h, m % 2] = value
                else:
                    p2[q, m, h] = value
        for d in (2, 1, 3):
            direct(q, d).start()

    def gain_terms():
        @pl.loop(0, 8)
        def _(i):
            px, pyh = lax.div(i, 2), lax.rem(i, 2)
            total = jnp.zeros((16, slab), F32)
            for g in range(16):
                u = uown[i, g].astype(F32) + urecv[i, g].astype(F32)
                total = total + u * wall[px, pyh, g].astype(F32)
            at = pl.multiple_of(i * 2 * slab + parity_at, slab)
            row = jnp.sum(total, axis=0, keepdims=True) / gain_row(at, slab)
            if tiles < 8:
                hbuf[px, pyh] = jnp.zeros((8, 128), F32)
            for t in range(tiles):
                hbuf[px, pyh, t : t + 1, :] = row[:, t * 128 : (t + 1) * 128]

    def hx_copy(d):
        return remote(
            hbuf.at[xs[d]], hx.at[d], hx_s.at[d], hx_r.at[d], device(xs[d], y, z, core)
        )

    def pair_copy(q):
        return remote(zxsrc.at[q], zxrecv.at[q], zx_s.at[q], zx_r.at[q], device(x, y, zpair, core))

    def finish(q):
        own = xs[0] if q % 2 == 1 else ys[0]
        for d in (1, 2, 3):
            direct(q, d).wait_recv()

        def value(h):
            return (
                p2[q, own, h].astype(F32) + in2[q, 1, h].astype(F32)
                + in2[q, 2, h].astype(F32) + in2[q, 3, h].astype(F32)
            )

        zxsrc[q] = value(1 - zl).astype(BF16)
        pair_copy(q).start()
        zown[q] = value(zl)

    def pair_finish(q):
        pair_copy(q).wait_recv()
        value = (zown[q] + zxrecv[q].astype(F32)).astype(BF16)
        zsrc = (zsrc0, zsrc1)[q // 2]
        for t in range(tiles):
            zsrc[t, q % 2] = value[:, t * 128 : (t + 1) * 128]

    def z_there(d):
        there = lax.rem(zh + d, tiles)
        return there, device(x, y, there * 2 + zl, core)

    def z_copy(b, d):
        there, where = z_there(d)
        src, dst = ((zsrc0, zrecv0), (zsrc1, zrecv1))[b]
        n = b * tiles + d
        return remote(src.at[there], dst.at[d], z_s.at[n], z_r.at[n], where)

    def zh_copy(d):
        there, where = z_there(d)
        return remote(zhsrc.at[there], zhrecv.at[d], zh_s.at[d], zh_r.at[d], where)

    def z_send(b):
        @pl.loop(1, tiles)
        def _(d):
            z_copy(b, d).start()

    hc_copy = remote(hx.at[0, 1 - yh], hcross, hc_s, hc_r, cross)

    def gain_start():
        for k, d, e in z_sends:
            agz(k, d, e).wait_recv()
        gain_terms()
        for d in range(1, 4):
            hx_copy(d).start()

    def gain_cross():
        for d in range(1, 4):
            hx_copy(d).wait_recv()
        hx[0] = hbuf[x] + hx[1] + hx[2] + hx[3]
        hc_copy.start()

    hz_copy = remote(hpair.at[0], hpair.at[1], hz_s, hz_r, device(x, y, zpair, core))

    def gain_pair():
        hc_copy.wait_recv()
        hpair[0] = hx[0, yh] + hcross[...]
        hz_copy.start()

    def gain_z():
        hz_copy.wait_recv()
        both = hpair[0] + hpair[1]
        for t in range(tiles):
            zhsrc[t] = both[t : t + 1]

        @pl.loop(1, tiles)
        def _(d):
            zh_copy(d).start()

    combine(0)
    ring_open(0)
    combine(1)
    ring_open(1)
    from_x(0)
    from_x(1)
    agc(3).start()
    agc(1).start()
    combine(2)
    combine(3)
    from_cross(0)
    hear(1)
    tell(2)
    ring_relay(0)
    ring_relay(1)
    from_opposite()
    from_cross(3)
    from_cross(1)
    from_same(0)
    ring_close(0)
    ring_close(1)
    ring_open(2)
    ring_open(3)
    from_cross(2)
    from_same(3)
    from_same(1)
    from_same(2)
    ring_relay(2)
    ring_relay(3)
    hear(2)
    finish(0)
    finish(1)
    gain_start()
    pair_finish(0)
    pair_finish(1)
    z_send(0)
    ring_close(2)
    ring_close(3)
    gain_cross()
    finish(2)
    finish(3)
    gain_pair()
    pair_finish(2)
    pair_finish(3)
    z_send(1)
    gain_z()

    for d in range(1, 4):
        hx_copy(d).wait_send()
    for k in range(2):
        agx(1, k).wait_send()
        agx(3, k).wait_send()
        agf(k).wait_send()
    for d in range(4):
        agc(d).wait_send()
        ags(d).wait_send()
    for k, d, e in z_sends:
        agz(k, d, e).wait_send()
    exps.wait_send()
    hc_copy.wait_send()

    for q in range(4):
        core_copy(q).wait_send()
        for k in range(6):
            ring(q, k).wait_send()
        for d in range(1, 4):
            direct(q, d).wait_send()

    for q in range(4):
        pair_copy(q).wait_send()
    hz_copy.wait_send()

    mine = yl * 2 + zl
    fin[mine, 0:2] = zsrc0[zh].astype(F32)
    fin[mine, 2:4] = zsrc1[zh].astype(F32)
    fin[mine, 4] = jnp.zeros((16, 128), F32)
    fin[mine, 4, 0:1] = zhsrc[zh]

    for b in range(2):

        @pl.loop(1, tiles)
        def _(d):
            z_copy(b, d).wait_recv()
            if b == 0:
                fin[mine, 0:2] += zrecv0[d].astype(F32)
            else:
                fin[mine, 2:4] += zrecv1[d].astype(F32)

    @pl.loop(1, tiles)
    def _(d):
        zh_copy(d).wait_recv()
        fin[mine, 4, 0:1] += zhrecv[d]

    ends = [device(x, y, zpair, core), device(x, ysame, z, core), device(x, ysame, zpair, core)]
    fin_copies = [
        remote(fin.at[mine], fin.at[mine], fin_s.at[k], fin_r.at[k], ends[k]) for k in range(3)
    ]
    for copy in fin_copies:
        copy.start()

    for b in range(2):

        @pl.loop(1, tiles)
        def _(d):
            z_copy(b, d).wait_send()

    @pl.loop(1, tiles)
    def _(d):
        zh_copy(d).wait_send()

    for copy in fin_copies:
        copy.wait()
    place = zl * 2 + yl
    for q in range(4):
        block = fin[:, q].reshape(64, 128)
        outt[:, q * 64 : (q + 1) * 64] = block.T
    gw_ref[...] = outt[pl.ds(pl.multiple_of(place * 32, 32), 32), :]
    row = fin[mine, 4, 0:8] + fin[(1 - yl) * 2 + zl, 4, 0:8]
    gg_ref[...] = pltpu.roll(row, lax.rem(128 - place * 32, 128), 1)[0:1, 0:32]


def hand_over(gw_ref, gg_ref, gw_out, gg_out, sem):
    copies = [
        pltpu.make_async_copy(gw_ref, gw_out, sem.at[0]),
        pltpu.make_async_copy(gg_ref, gg_out, sem.at[1]),
    ]
    for copy in copies:
        copy.start()
    for copy in copies:
        copy.wait()


def body(tokens, cotangent, weight, gain, exponents):
    width = tokens.shape[1]
    nz = lax.axis_size("rep") // 2
    slab = width // 16
    dma = pltpu.SemaphoreType.DMA
    vmem = pltpu.VMEM
    scratch = [
        vmem((16, 128, slab), BF16),
        vmem((128, 256), BF16),
        vmem((slab, 256), BF16),
        vmem((width,), BF16),
        vmem((2, width), jnp.int32),
        vmem((2, width), jnp.int32),
        vmem((128, min(slab, 256)), F32),
        vmem((4, 2, 16, 16, slab), BF16),
        vmem((8, 16, 16, slab), BF16),
        vmem((8, 16, 16, slab), BF16),
        vmem((8, 16, 16, slab), BF16),
        vmem((4, 4, 2, 4, 16, slab), BF16),
        vmem((4, 4, 16, slab), BF16),
        vmem((4, 4, 16, slab), BF16),
        vmem((4, 2, 4, 16, slab), BF16),
        vmem((4, 2, 4, 16, slab), BF16),
        vmem((4, 4, 2, 16, slab), BF16),
        vmem((4, 4, 2, 16, slab), BF16),
        vmem((4, 2, 8, 128), F32),
        vmem((4, 2, 8, 128), F32),
        vmem((8, 128), F32),
        vmem((2, 8, 128), F32),
        vmem((4, 16, slab), BF16),
        vmem((4, 16, slab), BF16),
        vmem((4, 16, slab), F32),
        vmem((slab // 128, 2, 16, 128), BF16),
        vmem((slab // 128, 2, 16, 128), BF16),
        vmem((slab // 128, 2, 16, 128), BF16),
        vmem((slab // 128, 2, 16, 128), BF16),
        vmem((slab // 128, 1, 128), F32),
        vmem((slab // 128, 1, 128), F32),
        vmem((4, 5, 16, 128), F32),
        vmem((128, 256), F32),
        pltpu.SemaphoreType.REGULAR((3,)),
        dma((4,)), dma((16,)), dma((4,)), dma((4,)), dma, dma,
        dma((4,)), dma((4,)), dma((2,)), dma((2,)), dma((4,)), dma((4,)), dma((4,)), dma((4,)),
        dma((16,)), dma((16,)),
        dma((24,)), dma((24,)), dma((16,)), dma((16,)), dma((4,)), dma((4,)), dma, dma,
        dma, dma, dma((4,)), dma((4,)),
        dma((slab // 64,)), dma((slab // 64,)), dma((slab // 128,)), dma((slab // 128,)), dma((3,)), dma((3,)),
    ]
    any_space = pl.BlockSpec(memory_space=pl.ANY)
    grad_weight, grad_gain = pl.pallas_call(
        functools.partial(kernel, width, slab, nz),
        out_shape=(
            jax.ShapeDtypeStruct((32, 256), F32),
            jax.ShapeDtypeStruct((1, 32), F32),
        ),
        in_specs=[any_space] * 5,
        out_specs=(pl.BlockSpec(memory_space=pltpu.VMEM),) * 2,
        scratch_shapes=scratch,
        compiler_params=pltpu.CompilerParams(
            collective_id=0, has_side_effects=True, vmem_limit_bytes=60 * 2**20
        ),
    )(tokens, cotangent, weight, gain, exponents.reshape(2, width))
    grad_weight, grad_gain = pl.pallas_call(
        hand_over,
        out_shape=(
            jax.ShapeDtypeStruct((32, 256), F32),
            jax.ShapeDtypeStruct((1, 32), F32),
        ),
        in_specs=[any_space] * 2,
        out_specs=(any_space,) * 2,
        scratch_shapes=[dma((2,))],
        compiler_params=pltpu.CompilerParams(vmem_limit_bytes=60 * 2**20),
    )(grad_weight, grad_gain)
    return (grad_weight, grad_gain.reshape(32))


def solution(mesh):
    placed = (
        P(("node", "rep"), None),
        P(("node", "rep"), None),
        P("node", None),
        P(),
        P("node", "rep", None, None),
    )
    return jax.shard_map(
        body,
        mesh=mesh,
        in_specs=placed,
        out_specs=(P(("node", "rep"), None), P(("node", "rep"))),
        check_vma=False,
    )
```
